256 devices in a mesh: cls: 32 (over x, y, core), feat: 8 (over z).
Axes of the slice: x: 4, y: 4, z: 8, core: 2. Of those that a mesh axis runs over, the one named last changes fastest.
Arguments:
- hidden_states: bfloat16 [512, 4096], P(None, 'feat'), may hold values from -24 to 24
- weight: bfloat16 [131072, 4096], P('cls', 'feat'), may hold values from -0.87890625 to 0.87890625
- target: int32 [512], replicated, may hold values from 0 to 131071
- row_moment: float32 [131072], P('cls'), may hold values from 1e-14 to 0.01
- col_moment: float32 [4096], P('feat'), may hold values from 0.002 to 0.008
Outputs:
- input_grad: bfloat16 [512, 4096], P(None, 'feat')
- row_loss: float32 [512], P('feat')
- new_weight: bfloat16 [131072, 4096], P('cls', 'feat')
- new_row_moment: float32 [131072], P('cls')
- new_col_moment: float32 [4096], P('feat')
The draws below stay inside these ranges and needn't reach their ends.
All inputs are finite; a program needn't handle non-finite values.
Results may differ from the reference program's by a relative error of at most 0.0004.
The reference program's roundings to bfloat16 on the way (of `dlogits`) count: a program that leaves them out, or rounds other values in their place, can miss the bound.
Values may be sent and summed in bfloat16 or wider, within the bound.
A program may use at most 128 MiB of HBM per device.

```python
import math
import jax
import jax.numpy as jnp
from jax import lax

D = 4096
V = 131072
ROWS = 512


def shared_rows(key):
    normal_rows = jnp.clip(jax.random.normal(jax.random.fold_in(key, 11), (ROWS, D), jnp.float32), -6.0, 6.0)
    return normal_rows


def draw_hidden_states(key, part):
    normal_rows = shared_rows(key)
    return normal_rows.astype(jnp.bfloat16)


def draw_weight(key, part):
    matrix = jnp.clip(jax.random.normal(jax.random.fold_in(key, 15), (V, D), jnp.float32), -6.0, 6.0) * (3.0 / math.sqrt(D))
    return matrix.astype(jnp.bfloat16)


def draw_row_moment(key, part):
    position = jnp.arange(V, dtype=jnp.float32) / V
    fresh_share = 0.03 + 0.94 * position * position
    chooser = jax.random.uniform(jax.random.fold_in(key, 21), (V,), jnp.float32, 0.0, 1.0)
    low_part = jax.random.uniform(jax.random.fold_in(key, 22), (V,), jnp.float32, 0.0, 0.35)
    high_part = jax.random.uniform(jax.random.fold_in(key, 23), (V,), jnp.float32, 0.75, 1.0)
    fraction = jnp.where(chooser < fresh_share, low_part, high_part)
    fraction = fraction.at[0].set(0.0)
    fraction = fraction.at[V - 1].set(1.0)
    low_log = math.log(1e-14)
    high_log = math.log(0.01)
    return jnp.clip(jnp.exp(low_log + fraction * (high_log - low_log)), 1e-14, 0.01).astype(jnp.float32)


def touch_ends(drawn, own_key, least, largest):
    place = [jax.random.randint(jax.random.fold_in(own_key, axis), (), 0, length) for axis, length in enumerate(drawn.shape)]
    main_axis = drawn.shape.index(max(drawn.shape))
    next_to = place[:main_axis] + [(place[main_axis] + 1) % drawn.shape[main_axis]] + place[main_axis + 1:]
    return drawn.at[tuple(place)].set(least).at[tuple(next_to)].set(largest)


def shard_levels(stream_key, dims, shards, least, largest):
    factor_of, own = 1.0, jax.random.fold_in(stream_key, 6)
    for dim, shards_of in shards:
        draws = jnp.exp(jax.random.uniform(jax.random.fold_in(own, dim), (shards_of,), jnp.float32, least / len(shards), largest / len(shards)))
        factor_of = factor_of * jnp.repeat(draws, dims[dim] // shards_of).reshape([-1 if axis == dim else 1 for axis in range(len(dims))])
    return factor_of


def setup_inputs(seed: int = 0) -> dict:
    key_of = jax.random.split(jax.random.key(seed), 6)
    hidden_states = draw_hidden_states(jax.random.fold_in(key_of[5], 71), 0)
    weight = draw_weight(jax.random.fold_in(key_of[5], 71), 0)
    target = touch_ends(jax.random.randint(key_of[2], (ROWS,), 0, V), jax.random.fold_in(key_of[2], 1), 0, V - 1).astype(jnp.int32)
    row_moment = draw_row_moment(jax.random.fold_in(key_of[5], 71), 0)
    col_moment = jnp.clip(jnp.exp(math.log(0.008) - 1.3862944 * jax.random.uniform(key_of[4], (D,), jnp.float32) ** shard_levels(key_of[4], (D,), ((0, 8),), -0.2, 0.2)), 0.002, 0.008)
    return dict(hidden_states=hidden_states, weight=weight, target=target, row_moment=row_moment, col_moment=col_moment)


tiny_square = 1e-30
decay_rate = 0.4
step_size = 0.1
clip_limit = 0.1

def reference(hidden_states, weight, target, row_moment, col_moment):
    logits = lax.dot_general(hidden_states, weight, (((1,), (1,)), ((), ())), preferred_element_type=jnp.float32)
    row_top = lax.optimization_barrier(jnp.max(logits, axis=1))
    shifted = jnp.exp(logits - row_top[:, None])
    exp_total = lax.optimization_barrier(jnp.sum(shifted, axis=1))
    columns = lax.broadcasted_iota(jnp.int32, logits.shape, 1)
    target_mask = columns == target.astype(jnp.int32)[:, None]
    picked = lax.optimization_barrier(jnp.sum(jnp.where(target_mask, logits, jnp.float32(0.0)), axis=1))
    row_loss = jnp.log(exp_total) + row_top - picked
    dlogits = (shifted / exp_total[:, None] - target_mask.astype(jnp.float32)).astype(jnp.bfloat16)
    input_grad = jnp.dot(dlogits, weight, preferred_element_type=jnp.float32).astype(jnp.bfloat16)
    weight_grad = lax.dot_general(dlogits, hidden_states, (((0,), (0,)), ((), ())), preferred_element_type=jnp.float32)
    squares = weight_grad * weight_grad + tiny_square
    new_row_moment = decay_rate * row_moment + (1.0 - decay_rate) * lax.optimization_barrier(jnp.mean(squares, axis=1))
    new_col_moment = decay_rate * col_moment + (1.0 - decay_rate) * lax.optimization_barrier(jnp.mean(squares, axis=0))
    update = weight_grad * lax.rsqrt(new_row_moment[:, None] * new_col_moment[None, :])
    update_rms = jnp.sqrt(jnp.mean(update * update))
    clip_scale = 1.0 / jnp.maximum(jnp.float32(1.0), update_rms / clip_limit)
    new_weight = (weight.astype(jnp.float32) - step_size * clip_scale * update).astype(jnp.bfloat16)
    return (input_grad, row_loss, new_weight, new_row_moment, new_col_moment)
```

```python
import jax
import jax.numpy as jnp
from jax import lax
from jax.sharding import PartitionSpec as P

D = 4096
V = 131072


tiny_square = 1e-30
decay_rate = 0.4
step_size = 0.1
clip_limit = 0.1


def on_device(hidden_states, weight, target, row_moment, col_moment):
    feat_count = lax.axis_size("feat")
    share_rows = hidden_states.shape[0] // feat_count
    local_classes = weight.shape[0]
    own_classes = local_classes // feat_count
    class_start = lax.axis_index("cls") * local_classes + lax.axis_index("feat") * own_classes
    row_offset = lax.axis_index("feat") * share_rows
    partial_value = lax.dot_general(
        weight, hidden_states, (((1,), (1,)), ((), ())), preferred_element_type=jnp.float32
    )
    logits = lax.psum_scatter(partial_value, "feat", scatter_dimension=0, tiled=True)
    classes = lax.broadcasted_iota(jnp.int32, (own_classes, 1), 0) + class_start
    target_mask = classes == target[None, :]
    local_picked = jnp.sum(jnp.where(target_mask, logits, jnp.float32(0.0)), axis=0)
    row_top = lax.pmax(jnp.max(logits, axis=0), ("cls", "feat"))
    shifted = jnp.exp(logits - row_top[None, :])
    exp_total, picked = lax.psum((jnp.sum(shifted, axis=0), local_picked), ("cls", "feat"))
    row_loss = jnp.log(exp_total) + row_top - picked
    own_dlogits = (shifted / exp_total[None, :] - target_mask.astype(jnp.float32)).astype(jnp.bfloat16)
    dlogits = lax.all_gather(own_dlogits, "feat", axis=0, tiled=True)
    own_loss = lax.dynamic_slice_in_dim(row_loss, row_offset, share_rows, 0)
    input_part = lax.dot_general(
        dlogits, weight, (((0,), (0,)), ((), ())), preferred_element_type=jnp.float32
    )
    weight_grad = jnp.dot(dlogits, hidden_states, preferred_element_type=jnp.float32)
    squares = weight_grad * weight_grad + tiny_square
    input_sum, col_sum = lax.psum((input_part, jnp.sum(squares, axis=0)), "cls")
    input_grad = input_sum.astype(jnp.bfloat16)
    row_sum = lax.psum(jnp.sum(squares, axis=1), "feat")
    new_row_moment = decay_rate * row_moment + (1.0 - decay_rate) * (row_sum / D)
    new_col_moment = decay_rate * col_moment + (1.0 - decay_rate) * (col_sum / V)
    update = weight_grad * lax.rsqrt(new_row_moment[:, None] * new_col_moment[None, :])
    update_square = lax.psum(jnp.sum(update * update), ("cls", "feat"))
    update_rms = jnp.sqrt(update_square / (V * D))
    clip_scale = 1.0 / jnp.maximum(jnp.float32(1.0), update_rms / clip_limit)
    new_weight = (weight.astype(jnp.float32) - step_size * clip_scale * update).astype(jnp.bfloat16)
    return (input_grad, own_loss, new_weight, new_row_moment, new_col_moment)


def solution(mesh):
    placed = (P(None, "feat"), P("cls", "feat"), P(), P("cls"), P("feat"))
    return jax.shard_map(
        on_device,
        mesh=mesh,
        in_specs=placed,
        out_specs=(P(None, "feat"), P("feat"), P("cls", "feat"), P("cls"), P("feat")),
        check_vma=False,
    )
```

```python
import functools

import jax
import jax.numpy as jnp
from jax import lax
from jax.experimental import pallas as pl
from jax.experimental.pallas import tpu as pltpu
from jax.sharding import PartitionSpec as P

MESH = pl.DeviceIdType.MESH
F32, BF16 = jnp.float32, jnp.bfloat16

TINY_SQUARE = 1e-30
DECAY = 0.4
STEP_SIZE = 0.1
CLIP_LIMIT = 0.1

GROUPS = 2
SUBS = 4


def kernel(
    sizes,
    h_ref, w_hbm, target_ref, rm_ref, cm_ref,
    ig_ref, loss_ref, nw_hbm, nrm_ref, ncm_ref,
    w, first, part, slot, logit, dl, grad, acc_in,
    stat_z, stat_c, rsum, rscale, csum, usum_z, usum_c, in_parts, in_out,
    w_sem, out_sem, rs_send, rs_recv, ag_send, ag_recv, st_send, st_recv, in_send, in_recv, mo_send, mo_recv,
):
    nz, nc, D, V = sizes
    z, cls = lax.axis_index("feat"), lax.axis_index("cls")
    chunk, width = w.shape[1], w.shape[2]
    rows = logit.shape[2]
    half = chunk // 2
    piece = half // SUBS
    quarter = chunk // 4

    def ring(i):
        return lax.rem(z + (i + 2 * nz), nz)

    up, down = {"feat": ring(1)}, {"feat": ring(-1)}
    side = (up, down)

    loads = [pltpu.make_async_copy(w_hbm.at[o], w.at[o], w_sem.at[o]) for o in range(nz)]
    for load in loads:
        load.start()

    barrier = pltpu.get_barrier_semaphore()

    def greet(axis, me, n):
        def body(j, c):
            pl.semaphore_signal(barrier, inc=1, device_id={axis: lax.rem(me + j, n)}, device_id_type=MESH)
            return c
        lax.fori_loop(1, n, body, 0)

    greet("feat", z, nz)
    greet("cls", cls, nc)
    pl.semaphore_wait(barrier, nz - 1 + nc - 1)
    for load in loads:
        load.wait()

    def spread(axis, me, n, src, dst, ssem, rsem):
        def body(j, c):
            pltpu.make_async_remote_copy(
                src, dst, ssem, rsem, device_id={axis: lax.rem(me + j, n)}, device_id_type=MESH
            ).start()
            return c
        lax.fori_loop(1, n, body, 0)

    def wait_bytes(ref, sem):
        pltpu.make_async_copy(ref, ref, sem).wait()

    def partial_logits(p, d, c):
        return lax.dot_general(
            w[c, half * d : half * (d + 1), :], h_ref[rows * p : rows * (p + 1), :],
            (((1,), (1,)), ((), ())), preferred_element_type=F32,
        )

    def rs_first(p):
        for d in range(2):
            c = ring(-1) if d == 0 else ring(1)
            first[p, d] = partial_logits(p, d, c).reshape(SUBS, piece, rows)
            for k in range(SUBS):
                pltpu.make_async_remote_copy(
                    first.at[p, d, k], slot.at[p, 0, d, k], rs_send.at[p, d], rs_recv.at[p, 0, d, k],
                    device_id=side[d], device_id_type=MESH,
                ).start()

    def rs_ticks(p, low, high):
        def tick(s, carry):
            for d in range(2):
                c = ring(-1 - s) if d == 0 else ring(1 + s)
                part[d] = partial_logits(p, d, c).reshape(SUBS, piece, rows)
            for k in range(SUBS):
                for d in range(2):
                    wait_bytes(slot.at[p, s - 1, d, k], rs_recv.at[p, s - 1, d, k])
                    slot[p, s - 1, d, k] = slot[p, s - 1, d, k] + part[d, k]
                    pltpu.make_async_remote_copy(
                        slot.at[p, s - 1, d, k], slot.at[p, s, d, k], rs_send.at[p, d], rs_recv.at[p, s, d, k],
                        device_id=side[d], device_id_type=MESH,
                    ).start()
            return carry
        lax.fori_loop(low, high, tick, 0)

    def rs_last(p):
        for d in range(2):
            part[d] = partial_logits(p, d, z).reshape(SUBS, piece, rows)
        for k in range(SUBS):
            for d in range(2):
                wait_bytes(slot.at[p, nz - 2, d, k], rs_recv.at[p, nz - 2, d, k])
                at = half * d + piece * k
                logit[p, at : at + piece, :] = slot[p, nz - 2, d, k] + part[d, k]

    def mask(p):
        classes = lax.broadcasted_iota(jnp.int32, (chunk, rows), 0) + (cls * (nz * chunk) + z * chunk)
        return classes == target_ref[:, rows * p : rows * (p + 1)]

    def pack(top, total, picked):
        row = lax.broadcasted_iota(jnp.int32, (8, rows), 0)
        return jnp.where(row == 0, top, jnp.where(row == 1, total, jnp.where(row == 2, picked, 0.0)))

    def combine(stats, n):
        top = stats[0][0:1]
        for j in range(1, n):
            top = jnp.maximum(top, stats[j][0:1])
        total, picked = jnp.zeros_like(top), jnp.zeros_like(top)
        for j in range(n):
            total = total + stats[j][1:2] * jnp.exp(stats[j][0:1] - top)
            picked = picked + stats[j][2:3]
        return top, total, picked

    def stats_local(p):
        values = logit[p]
        top = jnp.max(values, axis=0, keepdims=True)
        total = jnp.sum(jnp.exp(values - top), axis=0, keepdims=True)
        picked = jnp.sum(jnp.where(mask(p), values, 0.0), axis=0, keepdims=True)
        stat_z[p, z] = pack(top, total, picked)
        spread("feat", z, nz, stat_z.at[p, z], stat_z.at[p, z], st_send.at[p, 0], st_recv.at[p, 0])

    def stats_middle(p):
        wait_bytes(stat_z.at[p, pl.ds(0, nz - 1)], st_recv.at[p, 0])
        stat_c[p, cls] = pack(*combine([stat_z[p, j] for j in range(nz)], nz))
        spread("cls", cls, nc, stat_c.at[p, cls], stat_c.at[p, cls], st_send.at[p, 1], st_recv.at[p, 1])

    def stats_last(p):
        wait_bytes(stat_c.at[p, pl.ds(0, nc - 1)], st_recv.at[p, 1])
        top, total, picked = combine([stat_c[p, j] for j in range(nc)], nc)
        loss_ref[:, rows * p : rows * (p + 1)] = jnp.log(total) + top - picked
        soft = jnp.exp(logit[p] - top) / total - mask(p).astype(F32)
        dl[p, z] = soft.astype(BF16)

    def ag_copy(p, d, hop, k, c):
        part_of = dl.at[p, c, pl.ds(quarter * k, quarter)]
        return pltpu.make_async_remote_copy(
            part_of, part_of, ag_send.at[p], ag_recv.at[p, hop, d, k], device_id=side[d], device_id_type=MESH
        )

    def ag_first(p):
        for k in range(4):
            for d in range(2):
                ag_copy(p, d, 0, k, z).start()

    def ag_tick(p, t):
        for k in range(4):
            for d in range(2):
                c = ring(-t) if d == 0 else ring(t)
                if t < nz // 2 or (k < 2) == (d == 0):
                    ag_copy(p, d, t - 1, k, c).wait_recv()
                if t + 1 < nz // 2 or (t + 1 == nz // 2 and (k < 2) == (d == 0)):
                    ag_copy(p, d, t, k, c).start()

    def consume(p, c):
        for j in range(2):
            term = lax.dot_general(
                dl[p, c], w[c, :, (width // 2) * j : (width // 2) * (j + 1)],
                (((0,), (0,)), ((), ())), preferred_element_type=F32,
            )
            acc_in[p, j] = acc_in[p, j] + term

        def body(k, carry):
            at = pl.ds(pl.multiple_of(quarter * k, quarter), quarter)
            term = jnp.dot(dl[p, c, at, :], h_ref[rows * p : rows * (p + 1), :], preferred_element_type=F32)
            if p > 0:
                term = grad[c, at, :] + term
            grad[c, at, :] = term
            if p == GROUPS - 1:
                square = term * term + TINY_SQUARE
                column = square[0:8]
                for i in range(1, quarter // 8):
                    column = column + square[8 * i : 8 * (i + 1)]
                csum_acc = carry + column
                lanes = square[:, 0:128]
                for i in range(1, width // 128):
                    lanes = lanes + square[:, 128 * i : 128 * (i + 1)]
                rsum[z, pl.ds(4 * c + k, 1), :] = jnp.sum(lanes.T, axis=0, keepdims=True)
                return csum_acc
            return carry

        return lax.fori_loop(0, 4, body, jnp.zeros((8, width), F32))

    blocks = nc // 2
    high = rows // blocks

    def in_send_parts(p):
        def place(q):
            return acc_in.at[p, lax.rem(q, 2), pl.ds(pl.multiple_of((q // 2) * high, high), high), :]

        in_parts[p, cls] = place(cls)[...]

        def body(j, c):
            q = lax.rem(cls + j, nc)
            pltpu.make_async_remote_copy(
                place(q), in_parts.at[p, cls], in_send.at[p, 0], in_recv.at[p, 0],
                device_id={"cls": q}, device_id_type=MESH,
            ).start()
            return c
        lax.fori_loop(1, nc, body, 0)

    def in_sum(p):
        wait_bytes(in_parts.at[p, pl.ds(0, nc - 1)], in_recv.at[p, 0])
        total = in_parts[p, 0]
        for q in range(1, nc):
            total = total + in_parts[p, q]
        in_out[p, cls] = total.astype(BF16)
        spread("cls", cls, nc, in_out.at[p, cls], in_out.at[p, cls], in_send.at[p, 1], in_recv.at[p, 1])

    def in_store(p):
        wait_bytes(in_out.at[p, pl.ds(0, nc - 1)], in_recv.at[p, 1])
        for q in range(nc):
            at, j = rows * p + (q // 2) * high, q % 2
            ig_ref[at : at + high, (width // 2) * j : (width // 2) * (j + 1)] = in_out[p, q]

    acc_in[...] = jnp.zeros_like(acc_in)
    rs_first(0)
    rs_ticks(0, 1, nz - 1)
    rs_first(1)
    rs_last(0)
    stats_local(0)
    rs_ticks(1, 1, 2)
    stats_middle(0)
    rs_ticks(1, 2, 3)
    stats_last(0)
    rs_ticks(1, 3, nz - 1)
    ag_first(0)
    rs_last(1)
    stats_local(1)
    consume(0, z)
    ag_tick(0, 1)
    stats_middle(1)
    consume(0, ring(-1))
    consume(0, ring(1))
    ag_tick(0, 2)
    stats_last(1)
    ag_first(1)
    consume(0, ring(-2))
    consume(0, ring(2))
    ag_tick(0, 3)
    consume(0, ring(-3))
    consume(0, ring(3))
    ag_tick(0, 4)
    consume(0, ring(4))
    in_send_parts(0)
    column = consume(1, z)
    ag_tick(1, 1)
    column = column + consume(1, ring(-1))
    column = column + consume(1, ring(1))
    ag_tick(1, 2)
    in_sum(0)
    column = column + consume(1, ring(-2))
    column = column + consume(1, ring(2))
    ag_tick(1, 3)
    in_store(0)
    column = column + consume(1, ring(-3))
    column = column + consume(1, ring(3))
    ag_tick(1, 4)
    column = column + consume(1, ring(4))

    spread("feat", z, nz, rsum.at[z], rsum.at[z], mo_send.at[0], mo_recv.at[0])
    column = jnp.sum(column, axis=0, keepdims=True)
    for i in range(width // 128):
        csum[cls, i : i + 1, :] = column[:, 128 * i : 128 * (i + 1)]
    spread("cls", cls, nc, csum.at[cls], csum.at[cls], mo_send.at[1], mo_recv.at[1])
    in_send_parts(1)

    wait_bytes(rsum.at[pl.ds(0, nz - 1)], mo_recv.at[0])
    row_sum = rsum[0]
    for j in range(1, nz):
        row_sum = row_sum + rsum[j]
    new_rm = DECAY * rm_ref[...] + (1.0 - DECAY) * (row_sum / D)
    nrm_ref[...] = new_rm
    rscale[...] = lax.rsqrt(new_rm)
    wait_bytes(csum.at[pl.ds(0, nc - 1)], mo_recv.at[1])
    col_sum = csum[0]
    for j in range(1, nc):
        col_sum = col_sum + csum[j]
    for i in range(width // 128):
        ncm_ref[:, 128 * i : 128 * (i + 1)] = (
            DECAY * cm_ref[:, 128 * i : 128 * (i + 1)] + (1.0 - DECAY) * (col_sum[i : i + 1] / V)
        )
    col_scale = lax.rsqrt(ncm_ref[...])

    def scale(i, carry):
        c, k = i // 4, lax.rem(i, 4)
        at = pl.ds(pl.multiple_of(quarter * k, quarter), quarter)
        row_scale = jnp.broadcast_to(rscale[pl.ds(i, 1), :], (128, 128)).T
        for j in range(width // 128):
            lanes = slice(128 * j, 128 * (j + 1))
            update = grad[c, at, lanes] * row_scale * col_scale[:, lanes]
            grad[c, at, lanes] = update
            square = update * update
            for r in range(quarter // 8):
                carry = carry + square[8 * r : 8 * (r + 1)]
        return carry

    usum_z[z] = lax.fori_loop(0, 4 * nz, scale, jnp.zeros((8, 128), F32))
    spread("feat", z, nz, usum_z.at[z], usum_z.at[z], mo_send.at[2], mo_recv.at[2])
    in_sum(1)
    wait_bytes(usum_z.at[pl.ds(0, nz - 1)], mo_recv.at[2])
    total = usum_z[0]
    for j in range(1, nz):
        total = total + usum_z[j]
    usum_c[cls] = total
    spread("cls", cls, nc, usum_c.at[cls], usum_c.at[cls], mo_send.at[3], mo_recv.at[3])
    wait_bytes(usum_c.at[pl.ds(0, nc - 1)], mo_recv.at[3])
    total = usum_c[0]
    for j in range(1, nc):
        total = total + usum_c[j]
    update_square = jnp.sum(total, keepdims=True)
    update_rms = jnp.sqrt(update_square / (V * D))
    factor = STEP_SIZE * (1.0 / jnp.maximum(1.0, update_rms / CLIP_LIMIT))

    for o in range(nz):
        def write(k, carry, o=o):
            at = pl.ds(pl.multiple_of(quarter * k, quarter), quarter)
            w[o, at, :] = (w[o, at, :].astype(F32) - factor * grad[o, at, :]).astype(BF16)
            return carry
        lax.fori_loop(0, 4, write, 0)
        pltpu.make_async_copy(w.at[o], nw_hbm.at[o], out_sem.at[o]).start()
    in_store(1)

    for o in range(nz):
        pltpu.make_async_copy(w.at[o], nw_hbm.at[o], out_sem.at[o]).wait()
    for p in range(GROUPS):
        for d in range(2):
            wait_bytes(slot.at[p, :, d], rs_send.at[p, d])
        wait_bytes(dl.at[p, pl.ds(0, nz - 1)], ag_send.at[p])
        wait_bytes(stat_z.at[p, pl.ds(0, nz - 1)], st_send.at[p, 0])
        wait_bytes(stat_c.at[p, pl.ds(0, nc - 1)], st_send.at[p, 1])
        wait_bytes(in_parts.at[p, pl.ds(0, nc - 1)], in_send.at[p, 0])
        wait_bytes(in_out.at[p, pl.ds(0, nc - 1)], in_send.at[p, 1])
    wait_bytes(rsum.at[pl.ds(0, nz - 1)], mo_send.at[0])
    wait_bytes(csum.at[pl.ds(0, nc - 1)], mo_send.at[1])
    wait_bytes(usum_z.at[pl.ds(0, nz - 1)], mo_send.at[2])
    wait_bytes(usum_c.at[pl.ds(0, nc - 1)], mo_send.at[3])


def solution(mesh):
    nz, nc = mesh.shape["feat"], mesh.shape["cls"]

    def on_device(hidden, weight, target, row_moment, col_moment):
        all_rows, width = hidden.shape
        classes = weight.shape[0]
        rows, chunk = all_rows // GROUPS, classes // nz
        piece = chunk // 2 // SUBS
        sizes = (nz, nc, width * nz, classes * nc)
        vmem = pl.BlockSpec(memory_space=pltpu.VMEM)
        hbm = pl.BlockSpec(memory_space=pl.ANY)
        dma = pltpu.SemaphoreType.DMA
        high = rows // (nc // 2)
        input_grad, loss, new_weight, nrm, ncm = pl.pallas_call(
            functools.partial(kernel, sizes),
            out_shape=(
                jax.ShapeDtypeStruct((all_rows, width), BF16),
                jax.ShapeDtypeStruct((1, all_rows), F32),
                jax.ShapeDtypeStruct((nz, chunk, width), BF16),
                jax.ShapeDtypeStruct((classes // 128, 128), F32),
                jax.ShapeDtypeStruct((1, width), F32),
            ),
            in_specs=[vmem, hbm, vmem, vmem, vmem],
            out_specs=(vmem, vmem, hbm, vmem, vmem),
            scratch_shapes=[
                pltpu.VMEM((nz, chunk, width), BF16),
                pltpu.VMEM((GROUPS, 2, SUBS, piece, rows), F32),
                pltpu.VMEM((2, SUBS, piece, rows), F32),
                pltpu.VMEM((GROUPS, nz - 1, 2, SUBS, piece, rows), F32),
                pltpu.VMEM((GROUPS, chunk, rows), F32),
                pltpu.VMEM((GROUPS, nz, chunk, rows), BF16),
                pltpu.VMEM((nz, chunk, width), F32),
                pltpu.VMEM((GROUPS, 2, rows, width // 2), F32),
                pltpu.VMEM((GROUPS, nz, 8, rows), F32),
                pltpu.VMEM((GROUPS, nc, 8, rows), F32),
                pltpu.VMEM((nz, classes // 128, 128), F32),
                pltpu.VMEM((classes // 128, 128), F32),
                pltpu.VMEM((nc, 8, 128), F32),
                pltpu.VMEM((nz, 8, 128), F32),
                pltpu.VMEM((nc, 8, 128), F32),
                pltpu.VMEM((GROUPS, nc, high, width // 2), F32),
                pltpu.VMEM((GROUPS, nc, high, width // 2), BF16),
                dma((nz,)),
                dma((nz,)),
                dma((GROUPS, 2)),
                dma((GROUPS, nz - 1, 2, SUBS)),
                dma((GROUPS,)),
                dma((GROUPS, nz // 2, 2, 4)),
                dma((GROUPS, 2)),
                dma((GROUPS, 2)),
                dma((GROUPS, 2)),
                dma((GROUPS, 2)),
                dma((4,)),
                dma((4,)),
            ],
            compiler_params=pltpu.CompilerParams(
                collective_id=0, has_side_effects=True, vmem_limit_bytes=56 * 2**20
            ),
            cost_estimate=pl.CostEstimate(
                flops=6 * all_rows * classes * width, bytes_accessed=4 * classes * width, transcendentals=0
            ),
        )(
            hidden, weight.reshape(nz, chunk, width), target.reshape(1, all_rows),
            row_moment.reshape(classes // 128, 128), col_moment.reshape(1, width),
        )
        share = all_rows // nz
        own_loss = lax.dynamic_slice_in_dim(loss.reshape(all_rows), lax.axis_index("feat") * share, share, 0)
        return input_grad, own_loss, new_weight.reshape(classes, width), nrm.reshape(classes), ncm.reshape(width)

    return jax.shard_map(
        on_device,
        mesh=mesh,
        in_specs=(P(None, "feat"), P("cls", "feat"), P(), P("cls"), P("feat")),
        out_specs=(P(None, "feat"), P("feat"), P("cls", "feat"), P("cls"), P("feat")),
        check_vma=False,
    )
```

```python
import functools

import jax
import jax.numpy as jnp
from jax import lax
from jax.experimental import pallas as pl
from jax.experimental.pallas import tpu as pltpu
from jax.sharding import PartitionSpec as P

MESH = pl.DeviceIdType.MESH
F32, BF16 = jnp.float32, jnp.bfloat16

TINY_SQUARE = 1e-30
DECAY = 0.4
STEP_SIZE = 0.1
CLIP_LIMIT = 0.1

GROUPS = 2
SUBS = 4
LOW = 8
PER = 16 // LOW
MOST = 2.0 ** (15 + LOW) - 16.0


def kernel(
    sizes,
    h_ref, w_hbm, target_ref, rm_ref, cm_ref,
    ig_ref, loss_ref, nw_hbm, nrm_ref, ncm_ref,
    w, first, part, slot, bound, logit, dl, grad, acc_in,
    stat_z, stat_c, rsum, rscale, csum, usum_z, usum_c, in_parts, in_out,
    w_sem, out_sem, rs_send, rs_recv, bd_send, bd_recv, ag_send, ag_recv, st_send, st_recv, in_send, in_recv, mo_send, mo_recv,
):
    nz, nc, D, V = sizes
    z, cls = lax.axis_index("feat"), lax.axis_index("cls")
    chunk, width = w.shape[1], w.shape[2]
    rows = logit.shape[2]
    half = chunk // 2
    piece = half // SUBS
    quarter = chunk // 4

    def ring(i):
        return lax.rem(z + (i + 2 * nz), nz)

    up, down = {"feat": ring(1)}, {"feat": ring(-1)}
    side = (up, down)

    loads = [pltpu.make_async_copy(w_hbm.at[o], w.at[o], w_sem.at[o]) for o in range(nz)]
    for load in loads:
        load.start()

    barrier = pltpu.get_barrier_semaphore()

    def greet(axis, me, n):
        def body(j, c):
            pl.semaphore_signal(barrier, inc=1, device_id={axis: lax.rem(me + j, n)}, device_id_type=MESH)
            return c
        lax.fori_loop(1, n, body, 0)

    greet("feat", z, nz)
    greet("cls", cls, nc)
    pl.semaphore_wait(barrier, nz - 1 + nc - 1)
    for load in loads:
        load.wait()

    def spread(axis, me, n, src, dst, ssem, rsem):
        def body(j, c):
            pltpu.make_async_remote_copy(
                src, dst, ssem, rsem, device_id={axis: lax.rem(me + j, n)}, device_id_type=MESH
            ).start()
            return c
        lax.fori_loop(1, n, body, 0)

    def wait_bytes(ref, sem):
        pltpu.make_async_copy(ref, ref, sem).wait()

    def partial_logits(p, d, c):
        return lax.dot_general(
            w[c, half * d : half * (d + 1), :], h_ref[rows * p : rows * (p + 1), :],
            (((1,), (1,)), ((), ())), preferred_element_type=F32,
        )

    def encode(ref, value, top):
        number = jnp.round(value * (MOST / top)).astype(jnp.int32)
        ref[0:piece, :] = (number >> LOW).astype(jnp.int16)
        low = number & (2**LOW - 1)
        step = piece // PER
        word = low[0:step]
        for i in range(1, PER):
            word = word + (low[step * i : step * (i + 1)] << (LOW * i))
        ref[piece : piece + step, :] = (word - 32768).astype(jnp.int16)

    def decode(ref, top):
        high = ref[0:piece, :].astype(jnp.int32) << LOW
        word = ref[piece : piece + piece // PER, :].astype(jnp.int32) + 32768
        low = [(word >> (LOW * i)) & (2**LOW - 1) for i in range(PER)]
        return (high + jnp.concatenate(low, axis=0)).astype(F32) * (top * (1.0 / MOST))

    def largest(value):
        return jnp.max(jnp.abs(value), axis=0, keepdims=True)

    def bound_copy(p, s, d):
        return pltpu.make_async_remote_copy(
            bound.at[p, d, s, pl.ds(0, 1)], bound.at[p, d, s + 1, pl.ds(0, 1)], bd_send.at[p, d], bd_recv.at[p, s, d],
            device_id=side[d], device_id_type=MESH,
        )

    def rs_first(p):
        for d in range(2):
            c = ring(-1) if d == 0 else ring(1)
            value = partial_logits(p, d, c)
            top = jnp.maximum(largest(value), 1e-30)
            bound[p, d, 0, 0:1] = top
            bound_copy(p, 0, d).start()
            for k in range(SUBS):
                encode(first.at[p, d, k], value[piece * k : piece * (k + 1)], top)
                pltpu.make_async_remote_copy(
                    first.at[p, d, k], slot.at[p, 0, d, k], rs_send.at[p, d], rs_recv.at[p, 0, d, k],
                    device_id=side[d], device_id_type=MESH,
                ).start()

    def rs_ticks(p, low, high):
        def tick(s, carry):
            was, top = [], []
            for d in range(2):
                c = ring(-1 - s) if d == 0 else ring(1 + s)
                value = partial_logits(p, d, c)
                part[d] = value.reshape(SUBS, piece, rows)
                bound_copy(p, s - 1, d).wait_recv()
                was.append(bound[p, d, s, 0:1])
                top.append(was[d] + largest(value))
                bound[p, d, s, 0:1] = top[d]
                bound_copy(p, s, d).start()
            for k in range(SUBS):
                for d in range(2):
                    here = slot.at[p, s - 1, d, k]
                    wait_bytes(here, rs_recv.at[p, s - 1, d, k])
                    encode(here, decode(here, was[d]) + part[d, k], top[d])
                    pltpu.make_async_remote_copy(
                        here, slot.at[p, s, d, k], rs_send.at[p, d], rs_recv.at[p, s, d, k],
                        device_id=side[d], device_id_type=MESH,
                    ).start()
            return carry
        lax.fori_loop(low, high, tick, 0)

    def rs_last(p):
        for d in range(2):
            part[d] = partial_logits(p, d, z).reshape(SUBS, piece, rows)
            bound_copy(p, nz - 2, d).wait_recv()
        for k in range(SUBS):
            for d in range(2):
                wait_bytes(slot.at[p, nz - 2, d, k], rs_recv.at[p, nz - 2, d, k])
                at = half * d + piece * k
                logit[p, at : at + piece, :] = decode(slot.at[p, nz - 2, d, k], bound[p, d, nz - 1, 0:1]) + part[d, k]

    def mask(p):
        classes = lax.broadcasted_iota(jnp.int32, (chunk, rows), 0) + (cls * (nz * chunk) + z * chunk)
        return classes == target_ref[:, rows * p : rows * (p + 1)]

    def pack(top, total, picked):
        row = lax.broadcasted_iota(jnp.int32, (8, rows), 0)
        return jnp.where(row == 0, top, jnp.where(row == 1, total, jnp.where(row == 2, picked, 0.0)))

    def combine(stats, n):
        top = stats[0][0:1]
        for j in range(1, n):
            top = jnp.maximum(top, stats[j][0:1])
        total, picked = jnp.zeros_like(top), jnp.zeros_like(top)
        for j in range(n):
            total = total + stats[j][1:2] * jnp.exp(stats[j][0:1] - top)
            picked = picked + stats[j][2:3]
        return top, total, picked

    def stats_local(p):
        values = logit[p]
        top = jnp.max(values, axis=0, keepdims=True)
        total = jnp.sum(jnp.exp(values - top), axis=0, keepdims=True)
        picked = jnp.sum(jnp.where(mask(p), values, 0.0), axis=0, keepdims=True)
        stat_z[p, z] = pack(top, total, picked)
        spread("feat", z, nz, stat_z.at[p, z], stat_z.at[p, z], st_send.at[p, 0], st_recv.at[p, 0])

    def stats_middle(p):
        wait_bytes(stat_z.at[p, pl.ds(0, nz - 1)], st_recv.at[p, 0])
        stat_c[p, cls] = pack(*combine([stat_z[p, j] for j in range(nz)], nz))
        spread("cls", cls, nc, stat_c.at[p, cls], stat_c.at[p, cls], st_send.at[p, 1], st_recv.at[p, 1])

    def stats_last(p):
        wait_bytes(stat_c.at[p, pl.ds(0, nc - 1)], st_recv.at[p, 1])
        top, total, picked = combine([stat_c[p, j] for j in range(nc)], nc)
        loss_ref[:, rows * p : rows * (p + 1)] = jnp.log(total) + top - picked
        soft = jnp.exp(logit[p] - top) / total - mask(p).astype(F32)
        dl[p, z] = soft.astype(BF16)

    def ag_copy(p, d, hop, k, c):
        part_of = dl.at[p, c, pl.ds(quarter * k, quarter)]
        return pltpu.make_async_remote_copy(
            part_of, part_of, ag_send.at[p], ag_recv.at[p, hop, d, k], device_id=side[d], device_id_type=MESH
        )

    def ag_first(p):
        for k in range(4):
            for d in range(2):
                ag_copy(p, d, 0, k, z).start()

    def ag_tick(p, t):
        for k in range(4):
            for d in range(2):
                c = ring(-t) if d == 0 else ring(t)
                if t < nz // 2 or (k < 2) == (d == 0):
                    ag_copy(p, d, t - 1, k, c).wait_recv()
                if t + 1 < nz // 2 or (t + 1 == nz // 2 and (k < 2) == (d == 0)):
                    ag_copy(p, d, t, k, c).start()

    def consume(p, c):
        for j in range(2):
            term = lax.dot_general(
                dl[p, c], w[c, :, (width // 2) * j : (width // 2) * (j + 1)],
                (((0,), (0,)), ((), ())), preferred_element_type=F32,
            )
            acc_in[p, j] = acc_in[p, j] + term

        def body(k, carry):
            at = pl.ds(pl.multiple_of(quarter * k, quarter), quarter)
            term = jnp.dot(dl[p, c, at, :], h_ref[rows * p : rows * (p + 1), :], preferred_element_type=F32)
            if p > 0:
                term = grad[c, at, :] + term
            grad[c, at, :] = term
            if p == GROUPS - 1:
                square = term * term + TINY_SQUARE
                column = square[0:8]
                for i in range(1, quarter // 8):
                    column = column + square[8 * i : 8 * (i + 1)]
                csum_acc = carry + column
                lanes = square[:, 0:128]
                for i in range(1, width // 128):
                    lanes = lanes + square[:, 128 * i : 128 * (i + 1)]
                rsum[z, pl.ds(4 * c + k, 1), :] = jnp.sum(lanes.T, axis=0, keepdims=True)
                return csum_acc
            return carry

        return lax.fori_loop(0, 4, body, jnp.zeros((8, width), F32))

    blocks = nc // 2
    high = rows // blocks

    def in_send_parts(p):
        def place(q):
            return acc_in.at[p, lax.rem(q, 2), pl.ds(pl.multiple_of((q // 2) * high, high), high), :]

        in_parts[p, cls] = place(cls)[...]

        def body(j, c):
            q = lax.rem(cls + j, nc)
            pltpu.make_async_remote_copy(
                place(q), in_parts.at[p, cls], in_send.at[p, 0], in_recv.at[p, 0],
                device_id={"cls": q}, device_id_type=MESH,
            ).start()
            return c
        lax.fori_loop(1, nc, body, 0)

    def in_sum(p):
        wait_bytes(in_parts.at[p, pl.ds(0, nc - 1)], in_recv.at[p, 0])
        total = in_parts[p, 0]
        for q in range(1, nc):
            total = total + in_parts[p, q]
        in_out[p, cls] = total.astype(BF16)
        spread("cls", cls, nc, in_out.at[p, cls], in_out.at[p, cls], in_send.at[p, 1], in_recv.at[p, 1])

    def in_store(p):
        wait_bytes(in_out.at[p, pl.ds(0, nc - 1)], in_recv.at[p, 1])
        for q in range(nc):
            at, j = rows * p + (q // 2) * high, q % 2
            ig_ref[at : at + high, (width // 2) * j : (width // 2) * (j + 1)] = in_out[p, q]

    acc_in[...] = jnp.zeros_like(acc_in)
    rs_first(0)
    rs_ticks(0, 1, nz - 1)
    rs_first(1)
    rs_last(0)
    stats_local(0)
    rs_ticks(1, 1, 2)
    stats_middle(0)
    rs_ticks(1, 2, 3)
    stats_last(0)
    rs_ticks(1, 3, nz - 1)
    ag_first(0)
    rs_last(1)
    stats_local(1)
    consume(0, z)
    ag_tick(0, 1)
    stats_middle(1)
    consume(0, ring(-1))
    consume(0, ring(1))
    ag_tick(0, 2)
    stats_last(1)
    ag_first(1)
    consume(0, ring(-2))
    consume(0, ring(2))
    ag_tick(0, 3)
    consume(0, ring(-3))
    consume(0, ring(3))
    ag_tick(0, 4)
    consume(0, ring(4))
    in_send_parts(0)
    column = consume(1, z)
    ag_tick(1, 1)
    column = column + consume(1, ring(-1))
    column = column + consume(1, ring(1))
    ag_tick(1, 2)
    in_sum(0)
    column = column + consume(1, ring(-2))
    column = column + consume(1, ring(2))
    ag_tick(1, 3)
    in_store(0)
    column = column + consume(1, ring(-3))
    column = column + consume(1, ring(3))
    ag_tick(1, 4)
    column = column + consume(1, ring(4))

    spread("feat", z, nz, rsum.at[z], rsum.at[z], mo_send.at[0], mo_recv.at[0])
    column = jnp.sum(column, axis=0, keepdims=True)
    for i in range(width // 128):
        csum[cls, i : i + 1, :] = column[:, 128 * i : 128 * (i + 1)]
    spread("cls", cls, nc, csum.at[cls], csum.at[cls], mo_send.at[1], mo_recv.at[1])
    in_send_parts(1)

    wait_bytes(rsum.at[pl.ds(0, nz - 1)], mo_recv.at[0])
    row_sum = rsum[0]
    for j in range(1, nz):
        row_sum = row_sum + rsum[j]
    new_rm = DECAY * rm_ref[...] + (1.0 - DECAY) * (row_sum / D)
    nrm_ref[...] = new_rm
    rscale[...] = lax.rsqrt(new_rm)
    wait_bytes(csum.at[pl.ds(0, nc - 1)], mo_recv.at[1])
    col_sum = csum[0]
    for j in range(1, nc):
        col_sum = col_sum + csum[j]
    for i in range(width // 128):
        ncm_ref[:, 128 * i : 128 * (i + 1)] = (
            DECAY * cm_ref[:, 128 * i : 128 * (i + 1)] + (1.0 - DECAY) * (col_sum[i : i + 1] / V)
        )
    col_scale = lax.rsqrt(ncm_ref[...])

    def scale(i, carry):
        c, k = i // 4, lax.rem(i, 4)
        at = pl.ds(pl.multiple_of(quarter * k, quarter), quarter)
        row_scale = jnp.broadcast_to(rscale[pl.ds(i, 1), :], (128, 128)).T
        for j in range(width // 128):
            lanes = slice(128 * j, 128 * (j + 1))
            update = grad[c, at, lanes] * row_scale * col_scale[:, lanes]
            grad[c, at, lanes] = update
            square = update * update
            for r in range(quarter // 8):
                carry = carry + square[8 * r : 8 * (r + 1)]
        return carry

    usum_z[z] = lax.fori_loop(0, 4 * nz, scale, jnp.zeros((8, 128), F32))
    spread("feat", z, nz, usum_z.at[z], usum_z.at[z], mo_send.at[2], mo_recv.at[2])
    in_sum(1)
    wait_bytes(usum_z.at[pl.ds(0, nz - 1)], mo_recv.at[2])
    total = usum_z[0]
    for j in range(1, nz):
        total = total + usum_z[j]
    usum_c[cls] = total
    spread("cls", cls, nc, usum_c.at[cls], usum_c.at[cls], mo_send.at[3], mo_recv.at[3])
    wait_bytes(usum_c.at[pl.ds(0, nc - 1)], mo_recv.at[3])
    total = usum_c[0]
    for j in range(1, nc):
        total = total + usum_c[j]
    update_square = jnp.sum(total, keepdims=True)
    update_rms = jnp.sqrt(update_square / (V * D))
    factor = STEP_SIZE * (1.0 / jnp.maximum(1.0, update_rms / CLIP_LIMIT))

    for o in range(nz):
        def write(k, carry, o=o):
            at = pl.ds(pl.multiple_of(quarter * k, quarter), quarter)
            w[o, at, :] = (w[o, at, :].astype(F32) - factor * grad[o, at, :]).astype(BF16)
            return carry
        lax.fori_loop(0, 4, write, 0)
        pltpu.make_async_copy(w.at[o], nw_hbm.at[o], out_sem.at[o]).start()
    in_store(1)

    for o in range(nz):
        pltpu.make_async_copy(w.at[o], nw_hbm.at[o], out_sem.at[o]).wait()
    for p in range(GROUPS):
        for d in range(2):
            wait_bytes(slot.at[p, :, d], rs_send.at[p, d])
            wait_bytes(bound.at[p, d, pl.ds(0, nz - 1), pl.ds(0, 1)], bd_send.at[p, d])
        wait_bytes(dl.at[p, pl.ds(0, nz - 1)], ag_send.at[p])
        wait_bytes(stat_z.at[p, pl.ds(0, nz - 1)], st_send.at[p, 0])
        wait_bytes(stat_c.at[p, pl.ds(0, nc - 1)], st_send.at[p, 1])
        wait_bytes(in_parts.at[p, pl.ds(0, nc - 1)], in_send.at[p, 0])
        wait_bytes(in_out.at[p, pl.ds(0, nc - 1)], in_send.at[p, 1])
    wait_bytes(rsum.at[pl.ds(0, nz - 1)], mo_send.at[0])
    wait_bytes(csum.at[pl.ds(0, nc - 1)], mo_send.at[1])
    wait_bytes(usum_z.at[pl.ds(0, nz - 1)], mo_send.at[2])
    wait_bytes(usum_c.at[pl.ds(0, nc - 1)], mo_send.at[3])


def solution(mesh):
    nz, nc = mesh.shape["feat"], mesh.shape["cls"]

    def on_device(hidden, weight, target, row_moment, col_moment):
        all_rows, width = hidden.shape
        classes = weight.shape[0]
        rows, chunk = all_rows // GROUPS, classes // nz
        piece = chunk // 2 // SUBS
        words = piece + piece // PER
        sizes = (nz, nc, width * nz, classes * nc)
        vmem = pl.BlockSpec(memory_space=pltpu.VMEM)
        hbm = pl.BlockSpec(memory_space=pl.ANY)
        dma = pltpu.SemaphoreType.DMA
        high = rows // (nc // 2)
        input_grad, loss, new_weight, nrm, ncm = pl.pallas_call(
            functools.partial(kernel, sizes),
            out_shape=(
                jax.ShapeDtypeStruct((all_rows, width), BF16),
                jax.ShapeDtypeStruct((1, all_rows), F32),
                jax.ShapeDtypeStruct((nz, chunk, width), BF16),
                jax.ShapeDtypeStruct((classes // 128, 128), F32),
                jax.ShapeDtypeStruct((1, width), F32),
            ),
            in_specs=[vmem, hbm, vmem, vmem, vmem],
            out_specs=(vmem, vmem, hbm, vmem, vmem),
            scratch_shapes=[
                pltpu.VMEM((nz, chunk, width), BF16),
                pltpu.VMEM((GROUPS, 2, SUBS, words, rows), jnp.int16),
                pltpu.VMEM((2, SUBS, piece, rows), F32),
                pltpu.VMEM((GROUPS, nz - 1, 2, SUBS, words, rows), jnp.int16),
                pltpu.VMEM((GROUPS, 2, nz, 8, rows), F32),
                pltpu.VMEM((GROUPS, chunk, rows), F32),
                pltpu.VMEM((GROUPS, nz, chunk, rows), BF16),
                pltpu.VMEM((nz, chunk, width), F32),
                pltpu.VMEM((GROUPS, 2, rows, width // 2), F32),
                pltpu.VMEM((GROUPS, nz, 8, rows), F32),
                pltpu.VMEM((GROUPS, nc, 8, rows), F32),
                pltpu.VMEM((nz, classes // 128, 128), F32),
                pltpu.VMEM((classes // 128, 128), F32),
                pltpu.VMEM((nc, 8, 128), F32),
                pltpu.VMEM((nz, 8, 128), F32),
                pltpu.VMEM((nc, 8, 128), F32),
                pltpu.VMEM((GROUPS, nc, high, width // 2), F32),
                pltpu.VMEM((GROUPS, nc, high, width // 2), BF16),
                dma((nz,)),
                dma((nz,)),
                dma((GROUPS, 2)),
                dma((GROUPS, nz - 1, 2, SUBS)),
                dma((GROUPS, 2)),
                dma((GROUPS, nz - 1, 2)),
                dma((GROUPS,)),
                dma((GROUPS, nz // 2, 2, 4)),
                dma((GROUPS, 2)),
                dma((GROUPS, 2)),
                dma((GROUPS, 2)),
                dma((GROUPS, 2)),
                dma((4,)),
                dma((4,)),
            ],
            compiler_params=pltpu.CompilerParams(
                collective_id=0, has_side_effects=True, vmem_limit_bytes=56 * 2**20
            ),
            cost_estimate=pl.CostEstimate(
                flops=6 * all_rows * classes * width, bytes_accessed=4 * classes * width, transcendentals=0
            ),
        )(
            hidden, weight.reshape(nz, chunk, width), target.reshape(1, all_rows),
            row_moment.reshape(classes // 128, 128), col_moment.reshape(1, width),
        )
        share = all_rows // nz
        own_loss = lax.dynamic_slice_in_dim(loss.reshape(all_rows), lax.axis_index("feat") * share, share, 0)
        return input_grad, own_loss, new_weight.reshape(classes, width), nrm.reshape(classes), ncm.reshape(width)

    return jax.shard_map(
        on_device,
        mesh=mesh,
        in_specs=(P(None, "feat"), P("cls", "feat"), P(), P("cls"), P("feat")),
        out_specs=(P(None, "feat"), P("feat"), P("cls", "feat"), P("cls"), P("feat")),
        check_vma=False,
    )
```

```python
import functools

import jax
import jax.numpy as jnp
from jax import lax
from jax.experimental import pallas as pl
from jax.experimental.pallas import tpu as pltpu
from jax.sharding import PartitionSpec as P

MESH = pl.DeviceIdType.MESH
F32, BF16 = jnp.float32, jnp.bfloat16

TINY_SQUARE = 1e-30
DECAY = 0.4
STEP_SIZE = 0.1
CLIP_LIMIT = 0.1

GROUPS = 2
SUBS = 4
LOW = 8
PER = 16 // LOW
MOST = 2.0 ** (15 + LOW) - 16.0


def kernel(
    sizes,
    h_hbm, w_hbm, target_hbm, rm_hbm, cm_hbm,
    w, grad, ig_ref, loss_ref, nrm_ref, ncm_ref, factor_ref,
    h_ref, target_ref, rm_ref, cm_ref, first, part, slot, bound, logit, dl, acc_in,
    stat_z, stat_c, rsum, rscale, csum, usum_z, usum_c, in_parts, in_out,
    w_sem, rs_send, rs_recv, bd_send, bd_recv, ag_send, ag_recv, st_send, st_recv, in_send, in_recv, mo_send, mo_recv,
):
    nz, nc, D, V = sizes
    z, cls = lax.axis_index("feat"), lax.axis_index("cls")
    chunk, width = w.shape[1], w.shape[2]
    rows = logit.shape[2]
    half = chunk // 2
    piece = half // SUBS
    quarter = chunk // 4

    def ring(i):
        return lax.rem(z + (i + 2 * nz), nz)

    up, down = {"feat": ring(1)}, {"feat": ring(-1)}
    side = (up, down)

    loads = [pltpu.make_async_copy(h_hbm, h_ref, w_sem.at[nz])]
    loads += [pltpu.make_async_copy(w_hbm.at[o], w.at[o], w_sem.at[o]) for o in range(nz)]
    small = ((target_hbm, target_ref), (rm_hbm, rm_ref), (cm_hbm, cm_ref))
    loads += [pltpu.make_async_copy(a, b, w_sem.at[nz + 1 + i]) for i, (a, b) in enumerate(small)]
    for load in loads:
        load.start()

    barrier = pltpu.get_barrier_semaphore()

    def greet(axis, me, n):
        def body(j, c):
            pl.semaphore_signal(barrier, inc=1, device_id={axis: lax.rem(me + j, n)}, device_id_type=MESH)
            return c
        lax.fori_loop(1, n, body, 0)

    greet("feat", z, nz)
    greet("cls", cls, nc)
    pl.semaphore_wait(barrier, nz - 1 + nc - 1)
    for load in loads:
        load.wait()

    def spread(axis, me, n, src, dst, ssem, rsem):
        def body(j, c):
            pltpu.make_async_remote_copy(
                src, dst, ssem, rsem, device_id={axis: lax.rem(me + j, n)}, device_id_type=MESH
            ).start()
            return c
        lax.fori_loop(1, n, body, 0)

    def wait_bytes(ref, sem):
        pltpu.make_async_copy(ref, ref, sem).wait()

    def partial_logits(p, d, c):
        return lax.dot_general(
            w[c, half * d : half * (d + 1), :], h_ref[rows * p : rows * (p + 1), :],
            (((1,), (1,)), ((), ())), preferred_element_type=F32,
        )

    def encode(ref, value, top):
        number = jnp.round(value * (MOST / top)).astype(jnp.int32)
        ref[0:piece, :] = (number >> LOW).astype(jnp.int16)
        low = number & (2**LOW - 1)
        step = piece // PER
        word = low[0:step]
        for i in range(1, PER):
            word = word + (low[step * i : step * (i + 1)] << (LOW * i))
        ref[piece : piece + step, :] = (word - 32768).astype(jnp.int16)

    def decode(ref, top):
        high = ref[0:piece, :].astype(jnp.int32) << LOW
        word = ref[piece : piece + piece // PER, :].astype(jnp.int32) + 32768
        low = [(word >> (LOW * i)) & (2**LOW - 1) for i in range(PER)]
        return (high + jnp.concatenate(low, axis=0)).astype(F32) * (top * (1.0 / MOST))

    def largest(value):
        return jnp.max(jnp.abs(value), axis=0, keepdims=True)

    def bound_copy(p, s, d):
        return pltpu.make_async_remote_copy(
            bound.at[p, d, s, pl.ds(0, 1)], bound.at[p, d, s + 1, pl.ds(0, 1)], bd_send.at[p, d], bd_recv.at[p, s, d],
            device_id=side[d], device_id_type=MESH,
        )

    def rs_first(p):
        for d in range(2):
            c = ring(-1) if d == 0 else ring(1)
            value = partial_logits(p, d, c)
            top = jnp.maximum(largest(value), 1e-30)
            bound[p, d, 0, 0:1] = top
            bound_copy(p, 0, d).start()
            for k in range(SUBS):
                encode(first.at[p, d, k], value[piece * k : piece * (k + 1)], top)
                pltpu.make_async_remote_copy(
                    first.at[p, d, k], slot.at[p, 0, d, k], rs_send.at[p, d], rs_recv.at[p, 0, d, k],
                    device_id=side[d], device_id_type=MESH,
                ).start()

    def rs_ticks(p, low, high):
        def tick(s, carry):
            was, top = [], []
            for d in range(2):
                c = ring(-1 - s) if d == 0 else ring(1 + s)
                value = partial_logits(p, d, c)
                part[d] = value.reshape(SUBS, piece, rows)
                bound_copy(p, s - 1, d).wait_recv()
                was.append(bound[p, d, s, 0:1])
                top.append(was[d] + largest(value))
                bound[p, d, s, 0:1] = top[d]
                bound_copy(p, s, d).start()
            for k in range(SUBS):
                for d in range(2):
                    here = slot.at[p, s - 1, d, k]
                    wait_bytes(here, rs_recv.at[p, s - 1, d, k])
                    encode(here, decode(here, was[d]) + part[d, k], top[d])
                    pltpu.make_async_remote_copy(
                        here, slot.at[p, s, d, k], rs_send.at[p, d], rs_recv.at[p, s, d, k],
                        device_id=side[d], device_id_type=MESH,
                    ).start()
            return carry
        lax.fori_loop(low, high, tick, 0)

    def rs_last(p):
        for d in range(2):
            part[d] = partial_logits(p, d, z).reshape(SUBS, piece, rows)
            bound_copy(p, nz - 2, d).wait_recv()
        for k in range(SUBS):
            for d in range(2):
                wait_bytes(slot.at[p, nz - 2, d, k], rs_recv.at[p, nz - 2, d, k])
                at = half * d + piece * k
                logit[p, at : at + piece, :] = decode(slot.at[p, nz - 2, d, k], bound[p, d, nz - 1, 0:1]) + part[d, k]

    def mask(p):
        classes = lax.broadcasted_iota(jnp.int32, (chunk, rows), 0) + (cls * (nz * chunk) + z * chunk)
        return classes == target_ref[:, rows * p : rows * (p + 1)]

    def pack(top, total, picked):
        row = lax.broadcasted_iota(jnp.int32, (8, rows), 0)
        return jnp.where(row == 0, top, jnp.where(row == 1, total, jnp.where(row == 2, picked, 0.0)))

    def combine(stats, n):
        top = stats[0][0:1]
        for j in range(1, n):
            top = jnp.maximum(top, stats[j][0:1])
        total, picked = jnp.zeros_like(top), jnp.zeros_like(top)
        for j in range(n):
            total = total + stats[j][1:2] * jnp.exp(stats[j][0:1] - top)
            picked = picked + stats[j][2:3]
        return top, total, picked

    def stats_local(p):
        values = logit[p]
        top = jnp.max(values, axis=0, keepdims=True)
        total = jnp.sum(jnp.exp(values - top), axis=0, keepdims=True)
        picked = jnp.sum(jnp.where(mask(p), values, 0.0), axis=0, keepdims=True)
        stat_z[p, z] = pack(top, total, picked)
        spread("feat", z, nz, stat_z.at[p, z], stat_z.at[p, z], st_send.at[p, 0], st_recv.at[p, 0])

    def stats_middle(p):
        wait_bytes(stat_z.at[p, pl.ds(0, nz - 1)], st_recv.at[p, 0])
        stat_c[p, cls] = pack(*combine([stat_z[p, j] for j in range(nz)], nz))
        spread("cls", cls, nc, stat_c.at[p, cls], stat_c.at[p, cls], st_send.at[p, 1], st_recv.at[p, 1])

    def stats_last(p):
        wait_bytes(stat_c.at[p, pl.ds(0, nc - 1)], st_recv.at[p, 1])
        top, total, picked = combine([stat_c[p, j] for j in range(nc)], nc)
        loss_ref[:, rows * p : rows * (p + 1)] = jnp.log(total) + top - picked
        soft = jnp.exp(logit[p] - top) / total - mask(p).astype(F32)
        dl[p, z] = soft.astype(BF16)

    def ag_copy(p, d, hop, k, c):
        part_of = dl.at[p, c, pl.ds(quarter * k, quarter)]
        return pltpu.make_async_remote_copy(
            part_of, part_of, ag_send.at[p], ag_recv.at[p, hop, d, k], device_id=side[d], device_id_type=MESH
        )

    def ag_first(p):
        for k in range(4):
            for d in range(2):
                ag_copy(p, d, 0, k, z).start()

    def ag_tick(p, t, column=None):
        def take(d, k, column):
            c = ring(-t) if d == 0 else ring(t)
            ag_copy(p, d, t - 1, k, c).wait_recv()
            if t + 1 < nz // 2:
                ag_copy(p, d, t, k, c).start()
            elif t + 1 == nz // 2:
                @pl.when(k < 2 if d == 0 else k >= 2)
                def _():
                    ag_copy(p, d, t, k, c).start()
            return consume(p, c, k, column)

        def body(k, column):
            return take(1, k + 2 if t == nz // 2 else k, take(0, k, column))

        return lax.fori_loop(0, 2 if t == nz // 2 else 4, body, no_column if column is None else column)

    no_column = jnp.zeros((8, width), F32)

    def consume(p, c, k, column):
        at = pl.ds(pl.multiple_of(quarter * k, quarter), quarter)
        term = lax.dot_general(
            dl[p, c, at, :], w[c, at, :], (((0,), (0,)), ((), ())), preferred_element_type=F32
        )
        for j in range(2):
            acc_in[p, j] = acc_in[p, j] + term[:, (width // 2) * j : (width // 2) * (j + 1)]
        term = jnp.dot(dl[p, c, at, :], h_ref[rows * p : rows * (p + 1), :], preferred_element_type=F32)
        if p > 0:
            term = grad[c, at, :] + term
        grad[c, at, :] = term
        if p < GROUPS - 1:
            return column
        square = term * term + TINY_SQUARE
        for i in range(quarter // 8):
            column = column + square[8 * i : 8 * (i + 1)]
        lanes = square[:, 0:128]
        for i in range(1, width // 128):
            lanes = lanes + square[:, 128 * i : 128 * (i + 1)]
        rsum[z, pl.ds(4 * c + k, 1), :] = jnp.sum(lanes.T, axis=0, keepdims=True)
        return column

    def consume_own(p):
        return lax.fori_loop(0, 4, lambda k, column: consume(p, z, k, column), no_column)

    blocks = nc // 2
    high = rows // blocks

    def in_send_parts(p):
        def place(q):
            return acc_in.at[p, lax.rem(q, 2), pl.ds(pl.multiple_of((q // 2) * high, high), high), :]

        in_parts[p, cls] = place(cls)[...]

        def body(j, c):
            q = lax.rem(cls + j, nc)
            pltpu.make_async_remote_copy(
                place(q), in_parts.at[p, cls], in_send.at[p, 0], in_recv.at[p, 0],
                device_id={"cls": q}, device_id_type=MESH,
            ).start()
            return c
        lax.fori_loop(1, nc, body, 0)

    def in_sum(p):
        wait_bytes(in_parts.at[p, pl.ds(0, nc - 1)], in_recv.at[p, 0])
        total = in_parts[p, 0]
        for q in range(1, nc):
            total = total + in_parts[p, q]
        in_out[p, cls] = total.astype(BF16)
        spread("cls", cls, nc, in_out.at[p, cls], in_out.at[p, cls], in_send.at[p, 1], in_recv.at[p, 1])

    def in_store(p):
        wait_bytes(in_out.at[p, pl.ds(0, nc - 1)], in_recv.at[p, 1])
        for q in range(nc):
            at, j = rows * p + (q // 2) * high, q % 2
            ig_ref[at : at + high, (width // 2) * j : (width // 2) * (j + 1)] = in_out[p, q]

    acc_in[...] = jnp.zeros_like(acc_in)
    rs_first(0)
    rs_ticks(0, 1, nz - 1)
    rs_first(1)
    rs_last(0)
    stats_local(0)
    rs_ticks(1, 1, 2)
    stats_middle(0)
    rs_ticks(1, 2, 3)
    stats_last(0)
    rs_ticks(1, 3, nz - 1)
    ag_first(0)
    rs_last(1)
    stats_local(1)
    consume_own(0)
    ag_tick(0, 1)
    stats_middle(1)
    ag_tick(0, 2)
    stats_last(1)
    ag_first(1)
    ag_tick(0, 3)
    column = consume_own(1)
    column = ag_tick(1, 1, column)
    ag_tick(0, 4)
    in_send_parts(0)
    column = ag_tick(1, 2, column)
    in_sum(0)
    column = ag_tick(1, 3, column)
    in_store(0)
    column = ag_tick(1, 4, column)

    spread("feat", z, nz, rsum.at[z], rsum.at[z], mo_send.at[0], mo_recv.at[0])
    column = jnp.sum(column, axis=0, keepdims=True)
    for i in range(width // 128):
        csum[cls, i : i + 1, :] = column[:, 128 * i : 128 * (i + 1)]
    spread("cls", cls, nc, csum.at[cls], csum.at[cls], mo_send.at[1], mo_recv.at[1])
    in_send_parts(1)

    wait_bytes(rsum.at[pl.ds(0, nz - 1)], mo_recv.at[0])
    row_sum = rsum[0]
    for j in range(1, nz):
        row_sum = row_sum + rsum[j]
    new_rm = DECAY * rm_ref[...] + (1.0 - DECAY) * (row_sum / D)
    nrm_ref[...] = new_rm
    rscale[...] = lax.rsqrt(new_rm)
    wait_bytes(csum.at[pl.ds(0, nc - 1)], mo_recv.at[1])
    col_sum = csum[0]
    for j in range(1, nc):
        col_sum = col_sum + csum[j]
    for i in range(width // 128):
        ncm_ref[:, 128 * i : 128 * (i + 1)] = (
            DECAY * cm_ref[:, 128 * i : 128 * (i + 1)] + (1.0 - DECAY) * (col_sum[i : i + 1] / V)
        )
    col_scale = lax.rsqrt(ncm_ref[...])

    def scale(i, carry):
        c, k = i // 4, lax.rem(i, 4)
        at = pl.ds(pl.multiple_of(quarter * k, quarter), quarter)
        row_scale = jnp.broadcast_to(rscale[pl.ds(i, 1), :], (128, 128)).T
        for j in range(width // 128):
            lanes = slice(128 * j, 128 * (j + 1))
            update = grad[c, at, lanes] * row_scale * col_scale[:, lanes]
            grad[c, at, lanes] = update
            square = update * update
            for r in range(quarter // 32):
                carry = carry + square[32 * r : 32 * (r + 1)]
        return carry

    squares = lax.fori_loop(0, 4 * nz, scale, jnp.zeros((32, 128), F32), unroll=2)
    usum_z[z] = squares[0:8] + squares[8:16] + (squares[16:24] + squares[24:32])
    spread("feat", z, nz, usum_z.at[z], usum_z.at[z], mo_send.at[2], mo_recv.at[2])
    in_sum(1)
    wait_bytes(usum_z.at[pl.ds(0, nz - 1)], mo_recv.at[2])
    total = usum_z[0]
    for j in range(1, nz):
        total = total + usum_z[j]
    usum_c[cls] = total
    spread("cls", cls, nc, usum_c.at[cls], usum_c.at[cls], mo_send.at[3], mo_recv.at[3])
    wait_bytes(usum_c.at[pl.ds(0, nc - 1)], mo_recv.at[3])
    total = usum_c[0]
    for j in range(1, nc):
        total = total + usum_c[j]
    update_square = jnp.sum(total, keepdims=True)
    update_rms = jnp.sqrt(update_square / (V * D))
    factor = STEP_SIZE * (1.0 / jnp.maximum(1.0, update_rms / CLIP_LIMIT))

    factor_ref[...] = jnp.broadcast_to(factor, factor_ref.shape)
    in_store(1)

    for p in range(GROUPS):
        for d in range(2):
            wait_bytes(slot.at[p, :, d], rs_send.at[p, d])
            wait_bytes(bound.at[p, d, pl.ds(0, nz - 1), pl.ds(0, 1)], bd_send.at[p, d])
        wait_bytes(dl.at[p, pl.ds(0, nz - 1)], ag_send.at[p])
        wait_bytes(stat_z.at[p, pl.ds(0, nz - 1)], st_send.at[p, 0])
        wait_bytes(stat_c.at[p, pl.ds(0, nc - 1)], st_send.at[p, 1])
        wait_bytes(in_parts.at[p, pl.ds(0, nc - 1)], in_send.at[p, 0])
        wait_bytes(in_out.at[p, pl.ds(0, nc - 1)], in_send.at[p, 1])
    wait_bytes(rsum.at[pl.ds(0, nz - 1)], mo_send.at[0])
    wait_bytes(csum.at[pl.ds(0, nc - 1)], mo_send.at[1])
    wait_bytes(usum_z.at[pl.ds(0, nz - 1)], mo_send.at[2])
    wait_bytes(usum_c.at[pl.ds(0, nc - 1)], mo_send.at[3])


def finish(share, w, update, ig_in, loss_in, nrm_in, ncm_in, factor_ref, ig_ref, loss_ref, nw_hbm, nrm_ref, ncm_ref, new_w, out_sem):
    nz, chunk, width = w.shape
    factor = factor_ref[0:1, 0:1]
    copies = [pltpu.make_async_copy(new_w.at[o], nw_hbm.at[o], out_sem.at[o]) for o in range(nz)]
    for o in range(nz):
        def write(k, carry, o=o):
            at = pl.ds(pl.multiple_of(64 * k, 64), 64)
            new_w[o, at, :] = (w[o, at, :].astype(F32) - factor * update[o, at, :]).astype(BF16)
            return carry
        lax.fori_loop(0, chunk // 64, write, 0)
        copies[o].start()
    ig_ref[...] = ig_in[...]
    rows = loss_in.shape[1]
    loss = jnp.broadcast_to(loss_in[...], (8, rows))
    loss_ref[...] = pltpu.roll(loss, lax.rem(rows - share * lax.axis_index("feat"), rows), 1)[0:1, 0:share]
    nrm_ref[...] = nrm_in[...]
    ncm_ref[...] = ncm_in[...]
    for copy in copies:
        copy.wait()


def solution(mesh):
    nz, nc = mesh.shape["feat"], mesh.shape["cls"]

    def on_device(hidden, weight, target, row_moment, col_moment):
        all_rows, width = hidden.shape
        classes = weight.shape[0]
        rows, chunk = all_rows // GROUPS, classes // nz
        piece = chunk // 2 // SUBS
        words = piece + piece // PER
        sizes = (nz, nc, width * nz, classes * nc)
        vmem = pl.BlockSpec(memory_space=pltpu.VMEM)
        hbm = pl.BlockSpec(memory_space=pl.ANY)
        dma = pltpu.SemaphoreType.DMA
        high = rows // (nc // 2)
        between = pl.pallas_call(
            functools.partial(kernel, sizes),
            out_shape=(
                pltpu.VMEM((nz, chunk, width), BF16),
                pltpu.VMEM((nz, chunk, width), F32),
                pltpu.VMEM((all_rows, width), BF16),
                pltpu.VMEM((1, all_rows), F32),
                pltpu.VMEM((classes // 128, 128), F32),
                pltpu.VMEM((1, width), F32),
                pltpu.VMEM((8, 128), F32),
            ),
            in_specs=[hbm] * 5,
            out_specs=(vmem,) * 7,
            scratch_shapes=[
                pltpu.VMEM((all_rows, width), BF16),
                pltpu.VMEM((1, all_rows), jnp.int32),
                pltpu.VMEM((classes // 128, 128), F32),
                pltpu.VMEM((1, width), F32),
                pltpu.VMEM((GROUPS, 2, SUBS, words, rows), jnp.int16),
                pltpu.VMEM((2, SUBS, piece, rows), F32),
                pltpu.VMEM((GROUPS, nz - 1, 2, SUBS, words, rows), jnp.int16),
                pltpu.VMEM((GROUPS, 2, nz, 8, rows), F32),
                pltpu.VMEM((GROUPS, chunk, rows), F32),
                pltpu.VMEM((GROUPS, nz, chunk, rows), BF16),
                pltpu.VMEM((GROUPS, 2, rows, width // 2), F32),
                pltpu.VMEM((GROUPS, nz, 8, rows), F32),
                pltpu.VMEM((GROUPS, nc, 8, rows), F32),
                pltpu.VMEM((nz, classes // 128, 128), F32),
                pltpu.VMEM((classes // 128, 128), F32),
                pltpu.VMEM((nc, 8, 128), F32),
                pltpu.VMEM((nz, 8, 128), F32),
                pltpu.VMEM((nc, 8, 128), F32),
                pltpu.VMEM((GROUPS, nc, high, width // 2), F32),
                pltpu.VMEM((GROUPS, nc, high, width // 2), BF16),
                dma((nz + 4,)),
                dma((GROUPS, 2)),
                dma((GROUPS, nz - 1, 2, SUBS)),
                dma((GROUPS, 2)),
                dma((GROUPS, nz - 1, 2)),
                dma((GROUPS,)),
                dma((GROUPS, nz // 2, 2, 4)),
                dma((GROUPS, 2)),
                dma((GROUPS, 2)),
                dma((GROUPS, 2)),
                dma((GROUPS, 2)),
                dma((4,)),
                dma((4,)),
            ],
            compiler_params=pltpu.CompilerParams(
                collective_id=0, has_side_effects=True, vmem_limit_bytes=51 * 2**20
            ),
            cost_estimate=pl.CostEstimate(
                flops=6 * all_rows * classes * width, bytes_accessed=4 * classes * width, transcendentals=0
            ),
        )(
            hidden, weight.reshape(nz, chunk, width), target.reshape(1, all_rows),
            row_moment.reshape(classes // 128, 128), col_moment.reshape(1, width),
        )
        share = all_rows // nz
        input_grad, loss, new_weight, nrm, ncm = pl.pallas_call(
            functools.partial(finish, share),
            out_shape=(
                jax.ShapeDtypeStruct((all_rows, width), BF16),
                jax.ShapeDtypeStruct((1, share), F32),
                jax.ShapeDtypeStruct((nz, chunk, width), BF16),
                jax.ShapeDtypeStruct((classes // 128, 128), F32),
                jax.ShapeDtypeStruct((1, width), F32),
            ),
            in_specs=[vmem] * 7,
            out_specs=(vmem, vmem, hbm, vmem, vmem),
            scratch_shapes=[pltpu.VMEM((nz, chunk, width), BF16), dma((nz,))],
            compiler_params=pltpu.CompilerParams(vmem_limit_bytes=36 * 2**20),
            cost_estimate=pl.CostEstimate(flops=2 * classes * width, bytes_accessed=2 * classes * width, transcendentals=0),
        )(*between)
        return input_grad, loss.reshape(share), new_weight.reshape(classes, width), nrm.reshape(classes), ncm.reshape(width)

    return jax.shard_map(
        on_device,
        mesh=mesh,
        in_specs=(P(None, "feat"), P("cls", "feat"), P(), P("cls"), P("feat")),
        out_specs=(P(None, "feat"), P("feat"), P("cls", "feat"), P("cls"), P("feat")),
        check_vma=False,
    )
```

```python
import functools

import jax
import jax.numpy as jnp
from jax import lax
from jax.experimental import pallas as pl
from jax.experimental.pallas import tpu as pltpu
from jax.sharding import PartitionSpec as P

MESH = pl.DeviceIdType.MESH
F32, BF16 = jnp.float32, jnp.bfloat16

TINY_SQUARE = 1e-30
DECAY = 0.4
STEP_SIZE = 0.1
CLIP_LIMIT = 0.1

GROUPS = 2
SUBS = 4
LAG = 2
LOW = 4
PER = 16 // LOW
MOST = 2.0 ** (15 + LOW) - 16.0


def kernel(
    sizes,
    h_hbm, w_hbm, target_hbm, rm_hbm, cm_hbm,
    w, grad, ig_ref, loss_ref, nrm_ref, ncm_ref, factor_ref,
    h_ref, target_ref, rm_ref, cm_ref, first, part, slot, bound, came, logit, dl, acc_in,
    stat_z, stat_c, rsum, rscale, csum, usum_z, usum_c, in_parts, in_out,
    w_sem, rs_send, rs_recv, bd_send, bd_recv, ag_send, ag_recv, st_send, st_recv, in_send, in_recv, mo_send, mo_recv,
):
    nz, nc, D, V = sizes
    z, cls = lax.axis_index("feat"), lax.axis_index("cls")
    chunk, width = w.shape[1], w.shape[2]
    rows = logit.shape[2]
    half = chunk // 2
    piece = half // SUBS
    quarter = chunk // 4

    def ring(i):
        return lax.rem(z + (i + 2 * nz), nz)

    up, down = {"feat": ring(1)}, {"feat": ring(-1)}
    side = (up, down)

    loads = [pltpu.make_async_copy(h_hbm, h_ref, w_sem.at[nz])]
    loads += [pltpu.make_async_copy(w_hbm.at[o], w.at[o], w_sem.at[o]) for o in range(nz)]
    small = ((target_hbm, target_ref), (rm_hbm, rm_ref), (cm_hbm, cm_ref))
    loads += [pltpu.make_async_copy(a, b, w_sem.at[nz + 1 + i]) for i, (a, b) in enumerate(small)]
    for load in loads:
        load.start()

    barrier = pltpu.get_barrier_semaphore()

    def greet(axis, me, n):
        def body(j, c):
            pl.semaphore_signal(barrier, inc=1, device_id={axis: lax.rem(me + j, n)}, device_id_type=MESH)
            return c
        lax.fori_loop(1, n, body, 0)

    greet("feat", z, nz)
    greet("cls", cls, nc)
    pl.semaphore_wait(barrier, nz - 1 + nc - 1)
    for load in loads:
        load.wait()

    def spread(axis, me, n, src, dst, ssem, rsem):
        def body(j, c):
            pltpu.make_async_remote_copy(
                src, dst, ssem, rsem, device_id={axis: lax.rem(me + j, n)}, device_id_type=MESH
            ).start()
            return c
        lax.fori_loop(1, n, body, 0)

    def wait_bytes(ref, sem):
        pltpu.make_async_copy(ref, ref, sem).wait()

    def partial_logits(p, d, c):
        return lax.dot_general(
            w[c, half * d : half * (d + 1), :], h_ref[rows * p : rows * (p + 1), :],
            (((1,), (1,)), ((), ())), preferred_element_type=F32,
        )

    def encode(value, top):
        number = jnp.round(value * (MOST / top)).astype(jnp.int32)
        low = number & (2**LOW - 1)
        step = piece // PER
        word = low[0:step] - 32768
        for i in range(1, PER):
            word = word + (low[step * i : step * (i + 1)] << (LOW * i))
        return (number >> LOW).astype(jnp.int16), word.astype(jnp.int16)

    def decode(ref, top):
        high = ref[0:piece, :].astype(jnp.int32) << LOW
        word = ref[piece : piece + piece // PER, :].astype(jnp.int32) + 32768
        low = [(word >> (LOW * i)) & (2**LOW - 1) for i in range(PER)]
        return (high + jnp.concatenate(low, axis=0)).astype(F32) * (top * (1.0 / MOST))

    def ring_send(p, s, k, refs, values):
        tops = [jnp.maximum(jnp.max(jnp.abs(value), axis=0, keepdims=True), 1e-30) for value in values]
        codes = [encode(value, top) for value, top in zip(values, tops)]
        for d in range(2):
            bound[p, d, s, pl.ds(k, 1)] = tops[d]
            refs[d][0:piece, :] = codes[d][0]
            refs[d][piece : piece + piece // PER, :] = codes[d][1]
        for d in range(2):
            pltpu.make_async_remote_copy(
                bound.at[p, d, s, pl.ds(k, 1)], came.at[p, d, s, pl.ds(k, 1)], bd_send.at[p, d], bd_recv.at[p, s, d, k],
                device_id=side[d], device_id_type=MESH,
            ).start()
            pltpu.make_async_remote_copy(
                refs[d], slot.at[p, s, d, k], rs_send.at[p, d], rs_recv.at[p, s, d, k],
                device_id=side[d], device_id_type=MESH,
            ).start()

    def ring_take(p, s, k):
        for d in range(2):
            wait_bytes(came.at[p, d, s, pl.ds(k, 1)], bd_recv.at[p, s, d, k])
            wait_bytes(slot.at[p, s, d, k], rs_recv.at[p, s, d, k])
        return [decode(slot.at[p, s, d, k], came[p, d, s, pl.ds(k, 1)]) + part[p, d, k] for d in range(2)]

    def rs_first(p):
        value = [partial_logits(p, d, ring(-1) if d == 0 else ring(1)) for d in range(2)]
        for k in range(SUBS):
            ring_send(p, 0, k, [first.at[p, d, k] for d in range(2)], [value[d][piece * k : piece * (k + 1)] for d in range(2)])

    def rs_tick(p, s):
        for d in range(2):
            c = ring(-1 - s) if d == 0 else ring(1 + s)
            part[p, d] = partial_logits(p, d, c).reshape(SUBS, piece, rows)
        for k in range(SUBS):
            ring_send(p, s, k, [slot.at[p, s - 1, d, k] for d in range(2)], ring_take(p, s - 1, k))

    def rs_ticks(p, low, high):
        lax.fori_loop(low, high, lambda s, carry: (rs_tick(p, s), carry)[1], 0)

    def rs_both(low, high, lag):
        def tick(s, carry):
            rs_tick(0, s)
            rs_tick(1, s - lag)
            return carry
        lax.fori_loop(low, high, tick, 0)

    def rs_last(p):
        for d in range(2):
            part[p, d] = partial_logits(p, d, z).reshape(SUBS, piece, rows)
        for k in range(SUBS):
            for d, value in enumerate(ring_take(p, nz - 2, k)):
                at = half * d + piece * k
                logit[p, at : at + piece, :] = value

    def mask(p):
        classes = lax.broadcasted_iota(jnp.int32, (chunk, rows), 0) + (cls * (nz * chunk) + z * chunk)
        return classes == target_ref[:, rows * p : rows * (p + 1)]

    def pack(top, total, picked):
        row = lax.broadcasted_iota(jnp.int32, (8, rows), 0)
        return jnp.where(row == 0, top, jnp.where(row == 1, total, jnp.where(row == 2, picked, 0.0)))

    def combine(stats, n):
        top = stats[0][0:1]
        for j in range(1, n):
            top = jnp.maximum(top, stats[j][0:1])
        total, picked = jnp.zeros_like(top), jnp.zeros_like(top)
        for j in range(n):
            total = total + stats[j][1:2] * jnp.exp(stats[j][0:1] - top)
            picked = picked + stats[j][2:3]
        return top, total, picked

    def stats_local(p):
        values = logit[p]
        top = jnp.max(values, axis=0, keepdims=True)
        total = jnp.sum(jnp.exp(values - top), axis=0, keepdims=True)
        picked = jnp.sum(jnp.where(mask(p), values, 0.0), axis=0, keepdims=True)
        stat_z[p, z] = pack(top, total, picked)
        spread("feat", z, nz, stat_z.at[p, z], stat_z.at[p, z], st_send.at[p, 0], st_recv.at[p, 0])

    def stats_middle(p):
        wait_bytes(stat_z.at[p, pl.ds(0, nz - 1)], st_recv.at[p, 0])
        stat_c[p, cls] = pack(*combine([stat_z[p, j] for j in range(nz)], nz))
        spread("cls", cls, nc, stat_c.at[p, cls], stat_c.at[p, cls], st_send.at[p, 1], st_recv.at[p, 1])

    def stats_last(p):
        wait_bytes(stat_c.at[p, pl.ds(0, nc - 1)], st_recv.at[p, 1])
        top, total, picked = combine([stat_c[p, j] for j in range(nc)], nc)
        loss_ref[:, rows * p : rows * (p + 1)] = jnp.log(total) + top - picked
        soft = jnp.exp(logit[p] - top) / total - mask(p).astype(F32)
        dl[p, z] = soft.astype(BF16)

    def ag_copy(p, d, hop, k, c):
        part_of = dl.at[p, c, pl.ds(quarter * k, quarter)]
        return pltpu.make_async_remote_copy(
            part_of, part_of, ag_send.at[p], ag_recv.at[p, hop, d, k], device_id=side[d], device_id_type=MESH
        )

    def ag_first(p):
        for k in range(4):
            for d in range(2):
                ag_copy(p, d, 0, k, z).start()

    def ag_tick(p, t, column=None):
        def take(d, k, column):
            c = ring(-t) if d == 0 else ring(t)
            ag_copy(p, d, t - 1, k, c).wait_recv()
            if t + 1 < nz // 2:
                ag_copy(p, d, t, k, c).start()
            elif t + 1 == nz // 2:
                @pl.when(k < 2 if d == 0 else k >= 2)
                def _():
                    ag_copy(p, d, t, k, c).start()
            return consume(p, c, k, column)

        def body(k, column):
            return take(1, k + 2 if t == nz // 2 else k, take(0, k, column))

        return lax.fori_loop(0, 2 if t == nz // 2 else 4, body, no_column if column is None else column)

    no_column = jnp.zeros((8, width), F32)

    def consume(p, c, k, column):
        at = pl.ds(pl.multiple_of(quarter * k, quarter), quarter)
        term = lax.dot_general(
            dl[p, c, at, :], w[c, at, :], (((0,), (0,)), ((), ())), preferred_element_type=F32
        )
        for j in range(2):
            acc_in[p, j] = acc_in[p, j] + term[:, (width // 2) * j : (width // 2) * (j + 1)]
        term = jnp.dot(dl[p, c, at, :], h_ref[rows * p : rows * (p + 1), :], preferred_element_type=F32)
        if p > 0:
            term = grad[c, at, :] + term
        grad[c, at, :] = term
        if p < GROUPS - 1:
            return column
        square = term * term + TINY_SQUARE
        for i in range(quarter // 8):
            column = column + square[8 * i : 8 * (i + 1)]
        lanes = square[:, 0:128]
        for i in range(1, width // 128):
            lanes = lanes + square[:, 128 * i : 128 * (i + 1)]
        rsum[z, pl.ds(4 * c + k, 1), :] = jnp.sum(lanes.T, axis=0, keepdims=True)
        return column

    def consume_own(p):
        return lax.fori_loop(0, 4, lambda k, column: consume(p, z, k, column), no_column)

    blocks = nc // 2
    high = rows // blocks

    def in_send_parts(p):
        def place(q):
            return acc_in.at[p, lax.rem(q, 2), pl.ds(pl.multiple_of((q // 2) * high, high), high), :]

        in_parts[p, cls] = place(cls)[...]

        def body(j, c):
            q = lax.rem(cls + j, nc)
            pltpu.make_async_remote_copy(
                place(q), in_parts.at[p, cls], in_send.at[p, 0], in_recv.at[p, 0],
                device_id={"cls": q}, device_id_type=MESH,
            ).start()
            return c
        lax.fori_loop(1, nc, body, 0)

    def in_sum(p):
        wait_bytes(in_parts.at[p, pl.ds(0, nc - 1)], in_recv.at[p, 0])
        total = in_parts[p, 0]
        for q in range(1, nc):
            total = total + in_parts[p, q]
        in_out[p, cls] = total.astype(BF16)
        spread("cls", cls, nc, in_out.at[p, cls], in_out.at[p, cls], in_send.at[p, 1], in_recv.at[p, 1])

    def in_store(p):
        wait_bytes(in_out.at[p, pl.ds(0, nc - 1)], in_recv.at[p, 1])
        for q in range(nc):
            at, j = rows * p + (q // 2) * high, q % 2
            ig_ref[at : at + high, (width // 2) * j : (width // 2) * (j + 1)] = in_out[p, q]

    acc_in[...] = jnp.zeros_like(acc_in)
    rs_first(0)
    rs_ticks(0, 1, LAG + 1)
    rs_first(1)
    rs_both(LAG + 1, nz - 1, LAG)
    rs_last(0)
    stats_local(0)
    rs_ticks(1, nz - 1 - LAG, nz - LAG)
    stats_middle(0)
    rs_ticks(1, nz - LAG, nz + 1 - LAG)
    stats_last(0)
    ag_first(0)
    rs_ticks(1, nz + 1 - LAG, nz - 1)
    rs_last(1)
    stats_local(1)
    consume_own(0)
    ag_tick(0, 1)
    stats_middle(1)
    ag_tick(0, 2)
    stats_last(1)
    ag_first(1)
    ag_tick(0, 3)
    column = consume_own(1)
    column = ag_tick(1, 1, column)
    ag_tick(0, 4)
    in_send_parts(0)
    column = ag_tick(1, 2, column)
    in_sum(0)
    column = ag_tick(1, 3, column)
    in_store(0)
    column = ag_tick(1, 4, column)

    spread("feat", z, nz, rsum.at[z], rsum.at[z], mo_send.at[0], mo_recv.at[0])
    column = jnp.sum(column, axis=0, keepdims=True)
    for i in range(width // 128):
        csum[cls, i : i + 1, :] = column[:, 128 * i : 128 * (i + 1)]
    spread("cls", cls, nc, csum.at[cls], csum.at[cls], mo_send.at[1], mo_recv.at[1])
    in_send_parts(1)

    wait_bytes(rsum.at[pl.ds(0, nz - 1)], mo_recv.at[0])
    row_sum = rsum[0]
    for j in range(1, nz):
        row_sum = row_sum + rsum[j]
    new_rm = DECAY * rm_ref[...] + (1.0 - DECAY) * (row_sum / D)
    nrm_ref[...] = new_rm
    rscale[...] = lax.rsqrt(new_rm)
    wait_bytes(csum.at[pl.ds(0, nc - 1)], mo_recv.at[1])
    col_sum = csum[0]
    for j in range(1, nc):
        col_sum = col_sum + csum[j]
    for i in range(width // 128):
        ncm_ref[:, 128 * i : 128 * (i + 1)] = (
            DECAY * cm_ref[:, 128 * i : 128 * (i + 1)] + (1.0 - DECAY) * (col_sum[i : i + 1] / V)
        )
    col_scale = lax.rsqrt(ncm_ref[...])

    def scale(i, carry):
        c, k = i // 4, lax.rem(i, 4)
        at = pl.ds(pl.multiple_of(quarter * k, quarter), quarter)
        row_scale = jnp.broadcast_to(rscale[pl.ds(i, 1), :], (128, 128)).T
        for j in range(width // 128):
            lanes = slice(128 * j, 128 * (j + 1))
            update = grad[c, at, lanes] * row_scale * col_scale[:, lanes]
            grad[c, at, lanes] = update
            square = update * update
            for r in range(quarter // 32):
                carry = carry + square[32 * r : 32 * (r + 1)]
        return carry

    squares = lax.fori_loop(0, 4 * nz, scale, jnp.zeros((32, 128), F32), unroll=2)
    usum_z[z] = squares[0:8] + squares[8:16] + (squares[16:24] + squares[24:32])
    spread("feat", z, nz, usum_z.at[z], usum_z.at[z], mo_send.at[2], mo_recv.at[2])
    in_sum(1)
    wait_bytes(usum_z.at[pl.ds(0, nz - 1)], mo_recv.at[2])
    total = usum_z[0]
    for j in range(1, nz):
        total = total + usum_z[j]
    usum_c[cls] = total
    spread("cls", cls, nc, usum_c.at[cls], usum_c.at[cls], mo_send.at[3], mo_recv.at[3])
    wait_bytes(usum_c.at[pl.ds(0, nc - 1)], mo_recv.at[3])
    total = usum_c[0]
    for j in range(1, nc):
        total = total + usum_c[j]
    update_square = jnp.sum(total, keepdims=True)
    update_rms = jnp.sqrt(update_square / (V * D))
    factor = STEP_SIZE * (1.0 / jnp.maximum(1.0, update_rms / CLIP_LIMIT))

    factor_ref[...] = jnp.broadcast_to(factor, factor_ref.shape)
    in_store(1)

    for p in range(GROUPS):
        for d in range(2):
            wait_bytes(slot.at[p, :, d], rs_send.at[p, d])
            wait_bytes(bound.at[p, d, pl.ds(0, nz - 1), pl.ds(0, SUBS)], bd_send.at[p, d])
        wait_bytes(dl.at[p, pl.ds(0, nz - 1)], ag_send.at[p])
        wait_bytes(stat_z.at[p, pl.ds(0, nz - 1)], st_send.at[p, 0])
        wait_bytes(stat_c.at[p, pl.ds(0, nc - 1)], st_send.at[p, 1])
        wait_bytes(in_parts.at[p, pl.ds(0, nc - 1)], in_send.at[p, 0])
        wait_bytes(in_out.at[p, pl.ds(0, nc - 1)], in_send.at[p, 1])
    wait_bytes(rsum.at[pl.ds(0, nz - 1)], mo_send.at[0])
    wait_bytes(csum.at[pl.ds(0, nc - 1)], mo_send.at[1])
    wait_bytes(usum_z.at[pl.ds(0, nz - 1)], mo_send.at[2])
    wait_bytes(usum_c.at[pl.ds(0, nc - 1)], mo_send.at[3])


def finish(share, w, update, ig_in, loss_in, nrm_in, ncm_in, factor_ref, ig_ref, loss_ref, nw_hbm, nrm_ref, ncm_ref, new_w, out_sem):
    nz, chunk, width = w.shape
    factor = factor_ref[0:1, 0:1]
    copies = [pltpu.make_async_copy(new_w.at[o], nw_hbm.at[o], out_sem.at[o]) for o in range(nz)]
    for o in range(nz):
        def write(k, carry, o=o):
            at = pl.ds(pl.multiple_of(64 * k, 64), 64)
            new_w[o, at, :] = (w[o, at, :].astype(F32) - factor * update[o, at, :]).astype(BF16)
            return carry
        lax.fori_loop(0, chunk // 64, write, 0)
        copies[o].start()
    ig_ref[...] = ig_in[...]
    rows = loss_in.shape[1]
    loss = jnp.broadcast_to(loss_in[...], (8, rows))
    loss_ref[...] = pltpu.roll(loss, lax.rem(rows - share * lax.axis_index("feat"), rows), 1)[0:1, 0:share]
    nrm_ref[...] = nrm_in[...]
    ncm_ref[...] = ncm_in[...]
    for copy in copies:
        copy.wait()


def solution(mesh):
    nz, nc = mesh.shape["feat"], mesh.shape["cls"]

    def on_device(hidden, weight, target, row_moment, col_moment):
        all_rows, width = hidden.shape
        classes = weight.shape[0]
        rows, chunk = all_rows // GROUPS, classes // nz
        piece = chunk // 2 // SUBS
        words = piece + piece // PER
        sizes = (nz, nc, width * nz, classes * nc)
        vmem = pl.BlockSpec(memory_space=pltpu.VMEM)
        hbm = pl.BlockSpec(memory_space=pl.ANY)
        dma = pltpu.SemaphoreType.DMA
        high = rows // (nc // 2)
        between = pl.pallas_call(
            functools.partial(kernel, sizes),
            out_shape=(
                pltpu.VMEM((nz, chunk, width), BF16),
                pltpu.VMEM((nz, chunk, width), F32),
                pltpu.VMEM((all_rows, width), BF16),
                pltpu.VMEM((1, all_rows), F32),
                pltpu.VMEM((classes // 128, 128), F32),
                pltpu.VMEM((1, width), F32),
                pltpu.VMEM((8, 128), F32),
            ),
            in_specs=[hbm] * 5,
            out_specs=(vmem,) * 7,
            scratch_shapes=[
                pltpu.VMEM((all_rows, width), BF16),
                pltpu.VMEM((1, all_rows), jnp.int32),
                pltpu.VMEM((classes // 128, 128), F32),
                pltpu.VMEM((1, width), F32),
                pltpu.VMEM((GROUPS, 2, SUBS, words, rows), jnp.int16),
                pltpu.VMEM((GROUPS, 2, SUBS, piece, rows), F32),
                pltpu.VMEM((GROUPS, nz - 1, 2, SUBS, words, rows), jnp.int16),
                pltpu.VMEM((GROUPS, 2, nz - 1, 8, rows), F32),
                pltpu.VMEM((GROUPS, 2, nz - 1, 8, rows), F32),
                pltpu.VMEM((GROUPS, chunk, rows), F32),
                pltpu.VMEM((GROUPS, nz, chunk, rows), BF16),
                pltpu.VMEM((GROUPS, 2, rows, width // 2), F32),
                pltpu.VMEM((GROUPS, nz, 8, rows), F32),
                pltpu.VMEM((GROUPS, nc, 8, rows), F32),
                pltpu.VMEM((nz, classes // 128, 128), F32),
                pltpu.VMEM((classes // 128, 128), F32),
                pltpu.VMEM((nc, 8, 128), F32),
                pltpu.VMEM((nz, 8, 128), F32),
                pltpu.VMEM((nc, 8, 128), F32),
                pltpu.VMEM((GROUPS, nc, high, width // 2), F32),
                pltpu.VMEM((GROUPS, nc, high, width // 2), BF16),
                dma((nz + 4,)),
                dma((GROUPS, 2)),
                dma((GROUPS, nz - 1, 2, SUBS)),
                dma((GROUPS, 2)),
                dma((GROUPS, nz - 1, 2, SUBS)),
                dma((GROUPS,)),
                dma((GROUPS, nz // 2, 2, 4)),
                dma((GROUPS, 2)),
                dma((GROUPS, 2)),
                dma((GROUPS, 2)),
                dma((GROUPS, 2)),
                dma((4,)),
                dma((4,)),
            ],
            compiler_params=pltpu.CompilerParams(
                collective_id=0, has_side_effects=True, vmem_limit_bytes=51 * 2**20
            ),
            cost_estimate=pl.CostEstimate(
                flops=6 * all_rows * classes * width, bytes_accessed=4 * classes * width, transcendentals=0
            ),
        )(
            hidden, weight.reshape(nz, chunk, width), target.reshape(1, all_rows),
            row_moment.reshape(classes // 128, 128), col_moment.reshape(1, width),
        )
        share = all_rows // nz
        input_grad, loss, new_weight, nrm, ncm = pl.pallas_call(
            functools.partial(finish, share),
            out_shape=(
                jax.ShapeDtypeStruct((all_rows, width), BF16),
                jax.ShapeDtypeStruct((1, share), F32),
                jax.ShapeDtypeStruct((nz, chunk, width), BF16),
                jax.ShapeDtypeStruct((classes // 128, 128), F32),
                jax.ShapeDtypeStruct((1, width), F32),
            ),
            in_specs=[vmem] * 7,
            out_specs=(vmem, vmem, hbm, vmem, vmem),
            scratch_shapes=[pltpu.VMEM((nz, chunk, width), BF16), dma((nz,))],
            compiler_params=pltpu.CompilerParams(vmem_limit_bytes=36 * 2**20),
            cost_estimate=pl.CostEstimate(flops=2 * classes * width, bytes_accessed=2 * classes * width, transcendentals=0),
        )(*between)
        return input_grad, loss.reshape(share), new_weight.reshape(classes, width), nrm.reshape(classes), ncm.reshape(width)

    return jax.shard_map(
        on_device,
        mesh=mesh,
        in_specs=(P(None, "feat"), P("cls", "feat"), P(), P("cls"), P("feat")),
        out_specs=(P(None, "feat"), P("feat"), P("cls", "feat"), P("cls"), P("feat")),
        check_vma=False,
    )
```

```python
import functools

import jax
import jax.numpy as jnp
from jax import lax
from jax.experimental import pallas as pl
from jax.experimental.pallas import tpu as pltpu
from jax.sharding import PartitionSpec as P

MESH = pl.DeviceIdType.MESH
F32, BF16 = jnp.float32, jnp.bfloat16

TINY_SQUARE = 1e-30
DECAY = 0.4
STEP_SIZE = 0.1
CLIP_LIMIT = 0.1

GROUPS = 2
SUBS = 4
LAG = 2
LOW = 4
PER = 16 // LOW
MOST = 2.0 ** (15 + LOW) - 16.0


def kernel(
    sizes,
    h_hbm, w_hbm, target_hbm, rm_hbm, cm_hbm,
    w, grad, ig_ref, loss_ref, nrm_ref, ncm_ref, factor_ref,
    h_ref, target_ref, rm_ref, cm_ref, first, part, slot, bound, came, logit, dl, acc_in,
    stat_z, stat_c, rsum, rscale, csum, usum_z, usum_c, in_parts, in_out,
    w_sem, rs_send, rs_recv, bd_send, bd_recv, ag_send, ag_recv, st_send, st_recv, in_send, in_recv, mo_send, mo_recv,
):
    nz, nc, D, V = sizes
    z, cls = lax.axis_index("feat"), lax.axis_index("cls")
    chunk, width = w.shape[1], w.shape[2]
    rows = logit.shape[2]
    half = chunk // 2
    piece = half // SUBS
    quarter = chunk // 4

    def ring(i):
        return lax.rem(z + (i + 2 * nz), nz)

    up, down = {"feat": ring(1)}, {"feat": ring(-1)}
    side = (up, down)

    barrier = pltpu.get_barrier_semaphore()

    def greet(axis, me, n):
        def body(j, c):
            pl.semaphore_signal(barrier, inc=1, device_id={axis: lax.rem(me + j, n)}, device_id_type=MESH)
            return c
        lax.fori_loop(1, n, body, 0)

    greet("feat", z, nz)
    greet("cls", cls, nc)
    loads = [pltpu.make_async_copy(h_hbm, h_ref, w_sem.at[nz])]
    loads += [pltpu.make_async_copy(w_hbm.at[o], w.at[o], w_sem.at[o]) for o in range(nz)]
    small = ((target_hbm, target_ref), (rm_hbm, rm_ref), (cm_hbm, cm_ref))
    loads += [pltpu.make_async_copy(a, b, w_sem.at[nz + 1 + i]) for i, (a, b) in enumerate(small)]
    for load in loads:
        load.start()
    for load in loads:
        load.wait()

    def spread(axis, me, n, src, dst, ssem, rsem):
        def body(j, c):
            pltpu.make_async_remote_copy(
                src, dst, ssem, rsem, device_id={axis: lax.rem(me + j, n)}, device_id_type=MESH
            ).start()
            return c
        lax.fori_loop(1, n, body, 0)

    def wait_bytes(ref, sem):
        pltpu.make_async_copy(ref, ref, sem).wait()

    def partial_logits(p, d, c):
        return lax.dot_general(
            w[c, half * d : half * (d + 1), :], h_ref[rows * p : rows * (p + 1), :],
            (((1,), (1,)), ((), ())), preferred_element_type=F32,
        )

    def encode(value, top):
        number = jnp.round(value * (MOST / top)).astype(jnp.int32)
        low = number & (2**LOW - 1)
        step = piece // PER
        word = low[0:step] - 32768
        for i in range(1, PER):
            word = word + (low[step * i : step * (i + 1)] << (LOW * i))
        return (number >> LOW).astype(jnp.int16), word.astype(jnp.int16)

    def decode(ref, top):
        high = ref[0:piece, :].astype(jnp.int32) << LOW
        word = ref[piece : piece + piece // PER, :].astype(jnp.int32) + 32768
        low = [(word >> (LOW * i)) & (2**LOW - 1) for i in range(PER)]
        return (high + jnp.concatenate(low, axis=0)).astype(F32) * (top * (1.0 / MOST))

    def ring_send(p, s, k, refs, values):
        ring_write(p, s, k, refs, values)
        ring_start(p, s, k, refs)

    def ring_write(p, s, k, refs, values):
        tops = [jnp.maximum(jnp.max(jnp.abs(value), axis=0, keepdims=True), 1e-30) for value in values]
        codes = [encode(value, top) for value, top in zip(values, tops)]
        for d in range(2):
            bound[p, d, s, pl.ds(k, 1)] = tops[d]
            refs[d][0:piece, :] = codes[d][0]
            refs[d][piece : piece + piece // PER, :] = codes[d][1]

    def ring_start(p, s, k, refs):
        for d in range(2):
            pltpu.make_async_remote_copy(
                bound.at[p, d, s, pl.ds(k, 1)], came.at[p, d, s, pl.ds(k, 1)], bd_send.at[p, d], bd_recv.at[p, s, d, k],
                device_id=side[d], device_id_type=MESH,
            ).start()
            pltpu.make_async_remote_copy(
                refs[d], slot.at[p, s, d, k], rs_send.at[p, d], rs_recv.at[p, s, d, k],
                device_id=side[d], device_id_type=MESH,
            ).start()

    def ring_take(p, s, k):
        for d in range(2):
            wait_bytes(came.at[p, d, s, pl.ds(k, 1)], bd_recv.at[p, s, d, k])
            wait_bytes(slot.at[p, s, d, k], rs_recv.at[p, s, d, k])
        return [decode(slot.at[p, s, d, k], came[p, d, s, pl.ds(k, 1)]) + part[p, d, k] for d in range(2)]

    def rs_first(p):
        value = [partial_logits(p, d, ring(-1) if d == 0 else ring(1)) for d in range(2)]
        for k in range(SUBS):
            ring_write(p, 0, k, [first.at[p, d, k] for d in range(2)], [value[d][piece * k : piece * (k + 1)] for d in range(2)])
        if p == 0:
            pl.semaphore_wait(barrier, nz - 1 + nc - 1)
        for k in range(SUBS):
            ring_start(p, 0, k, [first.at[p, d, k] for d in range(2)])

    def rs_tick(p, s):
        for d in range(2):
            c = ring(-1 - s) if d == 0 else ring(1 + s)
            part[p, d] = partial_logits(p, d, c).reshape(SUBS, piece, rows)
        for k in range(SUBS):
            ring_send(p, s, k, [slot.at[p, s - 1, d, k] for d in range(2)], ring_take(p, s - 1, k))

    def rs_ticks(p, low, high):
        lax.fori_loop(low, high, lambda s, carry: (rs_tick(p, s), carry)[1], 0)

    def rs_both(low, high, lag):
        def tick(s, carry):
            rs_tick(0, s)
            rs_tick(1, s - lag)
            return carry
        lax.fori_loop(low, high, tick, 0)

    def rs_last(p):
        for d in range(2):
            part[p, d] = partial_logits(p, d, z).reshape(SUBS, piece, rows)
        for k in range(SUBS):
            for d, value in enumerate(ring_take(p, nz - 2, k)):
                at = half * d + piece * k
                logit[p, at : at + piece, :] = value

    def mask(p):
        classes = lax.broadcasted_iota(jnp.int32, (chunk, rows), 0) + (cls * (nz * chunk) + z * chunk)
        return classes == target_ref[:, rows * p : rows * (p + 1)]

    def pack(top, total, picked):
        row = lax.broadcasted_iota(jnp.int32, (8, rows), 0)
        return jnp.where(row == 0, top, jnp.where(row == 1, total, jnp.where(row == 2, picked, 0.0)))

    def combine(stats, n):
        top = stats[0][0:1]
        for j in range(1, n):
            top = jnp.maximum(top, stats[j][0:1])
        total, picked = jnp.zeros_like(top), jnp.zeros_like(top)
        for j in range(n):
            total = total + stats[j][1:2] * jnp.exp(stats[j][0:1] - top)
            picked = picked + stats[j][2:3]
        return top, total, picked

    def stats_local(p):
        values = logit[p]
        top = jnp.max(values, axis=0, keepdims=True)
        total = jnp.sum(jnp.exp(values - top), axis=0, keepdims=True)
        picked = jnp.sum(jnp.where(mask(p), values, 0.0), axis=0, keepdims=True)
        stat_z[p, z] = pack(top, total, picked)
        spread("feat", z, nz, stat_z.at[p, z], stat_z.at[p, z], st_send.at[p, 0], st_recv.at[p, 0])

    def stats_middle(p):
        wait_bytes(stat_z.at[p, pl.ds(0, nz - 1)], st_recv.at[p, 0])
        stat_c[p, cls] = pack(*combine([stat_z[p, j] for j in range(nz)], nz))
        spread("cls", cls, nc, stat_c.at[p, cls], stat_c.at[p, cls], st_send.at[p, 1], st_recv.at[p, 1])

    def stats_last(p):
        wait_bytes(stat_c.at[p, pl.ds(0, nc - 1)], st_recv.at[p, 1])
        top, total, picked = combine([stat_c[p, j] for j in range(nc)], nc)
        loss_ref[:, rows * p : rows * (p + 1)] = jnp.log(total) + top - picked
        soft = jnp.exp(logit[p] - top) / total - mask(p).astype(F32)
        dl[p, z] = soft.astype(BF16)

    def ag_copy(p, d, hop, k, c):
        part_of = dl.at[p, c, pl.ds(quarter * k, quarter)]
        return pltpu.make_async_remote_copy(
            part_of, part_of, ag_send.at[p], ag_recv.at[p, hop, d, k], device_id=side[d], device_id_type=MESH
        )

    def ag_first(p):
        for k in range(4):
            for d in range(2):
                ag_copy(p, d, 0, k, z).start()

    def ag_tick(p, t, column=None):
        def take(d, k, column):
            c = ring(-t) if d == 0 else ring(t)
            ag_copy(p, d, t - 1, k, c).wait_recv()
            if t + 1 < nz // 2:
                ag_copy(p, d, t, k, c).start()
            elif t + 1 == nz // 2:
                @pl.when(k < 2 if d == 0 else k >= 2)
                def _():
                    ag_copy(p, d, t, k, c).start()
            return consume(p, c, k, column)

        def body(k, column):
            return take(1, k + 2 if t == nz // 2 else k, take(0, k, column))

        return lax.fori_loop(0, 2 if t == nz // 2 else 4, body, no_column if column is None else column)

    no_column = jnp.zeros((8, width), F32)

    def consume(p, c, k, column):
        at = pl.ds(pl.multiple_of(quarter * k, quarter), quarter)
        term = lax.dot_general(
            dl[p, c, at, :], w[c, at, :], (((0,), (0,)), ((), ())), preferred_element_type=F32
        )
        for j in range(2):
            acc_in[p, j] = acc_in[p, j] + term[:, (width // 2) * j : (width // 2) * (j + 1)]
        term = jnp.dot(dl[p, c, at, :], h_ref[rows * p : rows * (p + 1), :], preferred_element_type=F32)
        if p > 0:
            term = grad[c, at, :] + term
        grad[c, at, :] = term
        if p < GROUPS - 1:
            return column
        square = term * term + TINY_SQUARE
        for i in range(quarter // 8):
            column = column + square[8 * i : 8 * (i + 1)]
        lanes = square[:, 0:128]
        for i in range(1, width // 128):
            lanes = lanes + square[:, 128 * i : 128 * (i + 1)]
        rsum[z, pl.ds(4 * c + k, 1), :] = jnp.sum(lanes.T, axis=0, keepdims=True)
        return column

    def consume_own(p):
        return lax.fori_loop(0, 4, lambda k, column: consume(p, z, k, column), no_column)

    blocks = nc // 2
    high = rows // blocks

    def in_send_parts(p):
        def place(q):
            return acc_in.at[p, lax.rem(q, 2), pl.ds(pl.multiple_of((q // 2) * high, high), high), :]

        in_parts[p, cls] = place(cls)[...]

        def body(j, c):
            q = lax.rem(cls + j, nc)
            pltpu.make_async_remote_copy(
                place(q), in_parts.at[p, cls], in_send.at[p, 0], in_recv.at[p, 0],
                device_id={"cls": q}, device_id_type=MESH,
            ).start()
            return c
        lax.fori_loop(1, nc, body, 0)

    def in_sum(p):
        wait_bytes(in_parts.at[p, pl.ds(0, nc - 1)], in_recv.at[p, 0])
        total = in_parts[p, 0]
        for q in range(1, nc):
            total = total + in_parts[p, q]
        in_out[p, cls] = total.astype(BF16)
        spread("cls", cls, nc, in_out.at[p, cls], in_out.at[p, cls], in_send.at[p, 1], in_recv.at[p, 1])

    def in_store(p):
        wait_bytes(in_out.at[p, pl.ds(0, nc - 1)], in_recv.at[p, 1])
        for q in range(nc):
            at, j = rows * p + (q // 2) * high, q % 2
            ig_ref[at : at + high, (width // 2) * j : (width // 2) * (j + 1)] = in_out[p, q]

    acc_in[...] = jnp.zeros_like(acc_in)
    rs_first(0)
    rs_ticks(0, 1, LAG + 1)
    rs_first(1)
    rs_both(LAG + 1, nz - 1, LAG)
    rs_last(0)
    stats_local(0)
    rs_ticks(1, nz - 1 - LAG, nz - LAG)
    stats_middle(0)
    rs_ticks(1, nz - LAG, nz + 1 - LAG)
    stats_last(0)
    ag_first(0)
    rs_ticks(1, nz + 1 - LAG, nz - 1)
    rs_last(1)
    stats_local(1)
    consume_own(0)
    ag_tick(0, 1)
    stats_middle(1)
    ag_tick(0, 2)
    stats_last(1)
    ag_first(1)
    ag_tick(0, 3)
    column = consume_own(1)
    column = ag_tick(1, 1, column)
    ag_tick(0, 4)
    in_send_parts(0)
    column = ag_tick(1, 2, column)
    in_sum(0)
    column = ag_tick(1, 3, column)
    in_store(0)
    column = ag_tick(1, 4, column)

    spread("feat", z, nz, rsum.at[z], rsum.at[z], mo_send.at[0], mo_recv.at[0])
    column = jnp.sum(column, axis=0, keepdims=True)
    for i in range(width // 128):
        csum[cls, i : i + 1, :] = column[:, 128 * i : 128 * (i + 1)]
    spread("cls", cls, nc, csum.at[cls], csum.at[cls], mo_send.at[1], mo_recv.at[1])
    in_send_parts(1)

    wait_bytes(rsum.at[pl.ds(0, nz - 1)], mo_recv.at[0])
    row_sum = rsum[0]
    for j in range(1, nz):
        row_sum = row_sum + rsum[j]
    new_rm = DECAY * rm_ref[...] + (1.0 - DECAY) * (row_sum / D)
    nrm_ref[...] = new_rm
    rscale[...] = lax.rsqrt(new_rm)
    wait_bytes(csum.at[pl.ds(0, nc - 1)], mo_recv.at[1])
    col_sum = csum[0]
    for j in range(1, nc):
        col_sum = col_sum + csum[j]
    for i in range(width // 128):
        ncm_ref[:, 128 * i : 128 * (i + 1)] = (
            DECAY * cm_ref[:, 128 * i : 128 * (i + 1)] + (1.0 - DECAY) * (col_sum[i : i + 1] / V)
        )
    col_scale = lax.rsqrt(ncm_ref[...])

    def scale(i, carry):
        c, k = i // 4, lax.rem(i, 4)
        at = pl.ds(pl.multiple_of(quarter * k, quarter), quarter)
        row_scale = jnp.broadcast_to(rscale[pl.ds(i, 1), :], (128, 128)).T
        for j in range(width // 128):
            lanes = slice(128 * j, 128 * (j + 1))
            update = grad[c, at, lanes] * row_scale * col_scale[:, lanes]
            grad[c, at, lanes] = update
            square = update * update
            for r in range(quarter // 32):
                carry = carry + square[32 * r : 32 * (r + 1)]
        return carry

    squares = lax.fori_loop(0, 4 * nz, scale, jnp.zeros((32, 128), F32), unroll=4)
    usum_z[z] = squares[0:8] + squares[8:16] + (squares[16:24] + squares[24:32])
    spread("feat", z, nz, usum_z.at[z], usum_z.at[z], mo_send.at[2], mo_recv.at[2])
    in_sum(1)
    wait_bytes(usum_z.at[pl.ds(0, nz - 1)], mo_recv.at[2])
    total = usum_z[0]
    for j in range(1, nz):
        total = total + usum_z[j]
    usum_c[cls] = total
    spread("cls", cls, nc, usum_c.at[cls], usum_c.at[cls], mo_send.at[3], mo_recv.at[3])
    wait_bytes(usum_c.at[pl.ds(0, nc - 1)], mo_recv.at[3])
    total = usum_c[0]
    for j in range(1, nc):
        total = total + usum_c[j]
    update_square = jnp.sum(total, keepdims=True)
    update_rms = jnp.sqrt(update_square / (V * D))
    factor = STEP_SIZE * (1.0 / jnp.maximum(1.0, update_rms / CLIP_LIMIT))

    factor_ref[...] = jnp.broadcast_to(factor, factor_ref.shape)
    in_store(1)

    for p in range(GROUPS):
        for d in range(2):
            wait_bytes(slot.at[p, :, d], rs_send.at[p, d])
            wait_bytes(bound.at[p, d, pl.ds(0, nz - 1), pl.ds(0, SUBS)], bd_send.at[p, d])
        wait_bytes(dl.at[p, pl.ds(0, nz - 1)], ag_send.at[p])
        wait_bytes(stat_z.at[p, pl.ds(0, nz - 1)], st_send.at[p, 0])
        wait_bytes(stat_c.at[p, pl.ds(0, nc - 1)], st_send.at[p, 1])
        wait_bytes(in_parts.at[p, pl.ds(0, nc - 1)], in_send.at[p, 0])
        wait_bytes(in_out.at[p, pl.ds(0, nc - 1)], in_send.at[p, 1])
    wait_bytes(rsum.at[pl.ds(0, nz - 1)], mo_send.at[0])
    wait_bytes(csum.at[pl.ds(0, nc - 1)], mo_send.at[1])
    wait_bytes(usum_z.at[pl.ds(0, nz - 1)], mo_send.at[2])
    wait_bytes(usum_c.at[pl.ds(0, nc - 1)], mo_send.at[3])


def finish(share, w, update, ig, loss_in, nrm, ncm, factor_ref, ig_hbm, loss_hbm, nw_hbm, nrm_hbm, ncm_hbm, new_w, loss, out_sem):
    nz, chunk, width = w.shape
    factor = factor_ref[0:1, 0:1]
    rows = loss_in.shape[1]
    wide = jnp.broadcast_to(loss_in[...], (8, rows))
    loss[...] = pltpu.roll(wide, lax.rem(rows - share * lax.axis_index("feat"), rows), 1)[0:1, 0:share]
    others = ((ig, ig_hbm), (loss, loss_hbm), (nrm, nrm_hbm), (ncm, ncm_hbm))
    copies = [pltpu.make_async_copy(a, b, out_sem.at[nz + i]) for i, (a, b) in enumerate(others)]
    for copy in copies:
        copy.start()
    for o in range(nz):
        def write(k, carry, o=o):
            at = pl.ds(pl.multiple_of(64 * k, 64), 64)
            new_w[o, at, :] = (w[o, at, :].astype(F32) - factor * update[o, at, :]).astype(BF16)
            return carry
        lax.fori_loop(0, chunk // 64, write, 0)
        copies.append(pltpu.make_async_copy(new_w.at[o], nw_hbm.at[o], out_sem.at[o]))
        copies[-1].start()
    for copy in copies:
        copy.wait()


def solution(mesh):
    nz, nc = mesh.shape["feat"], mesh.shape["cls"]

    def on_device(hidden, weight, target, row_moment, col_moment):
        all_rows, width = hidden.shape
        classes = weight.shape[0]
        rows, chunk = all_rows // GROUPS, classes // nz
        piece = chunk // 2 // SUBS
        words = piece + piece // PER
        sizes = (nz, nc, width * nz, classes * nc)
        vmem = pl.BlockSpec(memory_space=pltpu.VMEM)
        hbm = pl.BlockSpec(memory_space=pl.ANY)
        dma = pltpu.SemaphoreType.DMA
        high = rows // (nc // 2)
        between = pl.pallas_call(
            functools.partial(kernel, sizes),
            out_shape=(
                pltpu.VMEM((nz, chunk, width), BF16),
                pltpu.VMEM((nz, chunk, width), F32),
                pltpu.VMEM((all_rows, width), BF16),
                pltpu.VMEM((1, all_rows), F32),
                pltpu.VMEM((classes // 128, 128), F32),
                pltpu.VMEM((1, width), F32),
                pltpu.VMEM((8, 128), F32),
            ),
            in_specs=[hbm] * 5,
            out_specs=(vmem,) * 7,
            scratch_shapes=[
                pltpu.VMEM((all_rows, width), BF16),
                pltpu.VMEM((1, all_rows), jnp.int32),
                pltpu.VMEM((classes // 128, 128), F32),
                pltpu.VMEM((1, width), F32),
                pltpu.VMEM((GROUPS, 2, SUBS, words, rows), jnp.int16),
                pltpu.VMEM((GROUPS, 2, SUBS, piece, rows), F32),
                pltpu.VMEM((GROUPS, nz - 1, 2, SUBS, words, rows), jnp.int16),
                pltpu.VMEM((GROUPS, 2, nz - 1, 8, rows), F32),
                pltpu.VMEM((GROUPS, 2, nz - 1, 8, rows), F32),
                pltpu.VMEM((GROUPS, chunk, rows), F32),
                pltpu.VMEM((GROUPS, nz, chunk, rows), BF16),
                pltpu.VMEM((GROUPS, 2, rows, width // 2), F32),
                pltpu.VMEM((GROUPS, nz, 8, rows), F32),
                pltpu.VMEM((GROUPS, nc, 8, rows), F32),
                pltpu.VMEM((nz, classes // 128, 128), F32),
                pltpu.VMEM((classes // 128, 128), F32),
                pltpu.VMEM((nc, 8, 128), F32),
                pltpu.VMEM((nz, 8, 128), F32),
                pltpu.VMEM((nc, 8, 128), F32),
                pltpu.VMEM((GROUPS, nc, high, width // 2), F32),
                pltpu.VMEM((GROUPS, nc, high, width // 2), BF16),
                dma((nz + 4,)),
                dma((GROUPS, 2)),
                dma((GROUPS, nz - 1, 2, SUBS)),
                dma((GROUPS, 2)),
                dma((GROUPS, nz - 1, 2, SUBS)),
                dma((GROUPS,)),
                dma((GROUPS, nz // 2, 2, 4)),
                dma((GROUPS, 2)),
                dma((GROUPS, 2)),
                dma((GROUPS, 2)),
                dma((GROUPS, 2)),
                dma((4,)),
                dma((4,)),
            ],
            compiler_params=pltpu.CompilerParams(
                collective_id=0, has_side_effects=True, vmem_limit_bytes=51 * 2**20
            ),
            cost_estimate=pl.CostEstimate(
                flops=6 * all_rows * classes * width, bytes_accessed=4 * classes * width, transcendentals=0
            ),
        )(
            hidden, weight.reshape(nz, chunk, width), target.reshape(1, all_rows),
            row_moment.reshape(classes // 128, 128), col_moment.reshape(1, width),
        )
        share = all_rows // nz
        input_grad, loss, new_weight, nrm, ncm = pl.pallas_call(
            functools.partial(finish, share),
            out_shape=(
                jax.ShapeDtypeStruct((all_rows, width), BF16),
                jax.ShapeDtypeStruct((1, share), F32),
                jax.ShapeDtypeStruct((nz, chunk, width), BF16),
                jax.ShapeDtypeStruct((classes // 128, 128), F32),
                jax.ShapeDtypeStruct((1, width), F32),
            ),
            in_specs=[vmem] * 7,
            out_specs=(hbm,) * 5,
            scratch_shapes=[pltpu.VMEM((nz, chunk, width), BF16), pltpu.VMEM((1, share), F32), dma((nz + 4,))],
            compiler_params=pltpu.CompilerParams(vmem_limit_bytes=36 * 2**20),
            cost_estimate=pl.CostEstimate(flops=2 * classes * width, bytes_accessed=2 * classes * width, transcendentals=0),
        )(*between)
        return input_grad, loss.reshape(share), new_weight.reshape(classes, width), nrm.reshape(classes), ncm.reshape(width)

    return jax.shard_map(
        on_device,
        mesh=mesh,
        in_specs=(P(None, "feat"), P("cls", "feat"), P(), P("cls"), P("feat")),
        out_specs=(P(None, "feat"), P("feat"), P("cls", "feat"), P("cls"), P("feat")),
        check_vma=False,
    )
```
